128 devices in a mesh: table: 8 (over y, core), dom: 16 (over z, x).
Axes of the slice: x: 4, y: 4, z: 4, core: 2. Of those that a mesh axis runs over, the one named last changes fastest.
Arguments:
- tables: float32 [8, 131072, 128], P('table', 'dom'), may hold values from -6 to 6
- owner_ids: int32 [65536, 4], P(('table', 'dom')), may hold values from 0 to 127, all different within a row; in each aligned block of 512 rows (0 to 511, 512 to 1023, ...) at most 32 rows name the same one
- row_ids: int32 [65536, 4], P(('table', 'dom')), may hold values from 0 to 8191
- neighbour_part: int32 [512, 4], P(('table', 'dom')), may hold values from 0 to 15, all different within a row; in each aligned block of 4 rows (0 to 3, 4 to 7, ...) at most 2 rows name the same one
- neighbour_block: int32 [512, 4], P(('table', 'dom')), may hold values from 0 to 3
- adjacency: bfloat16 [512, 4, 128, 128], P(('table', 'dom')), may hold values from 0.001 to 1.81
- w_in: bfloat16 [128, 1024], replicated, may hold values from -0.5 to 0.5
- w_pool: bfloat16 [1024, 1024], replicated, may hold values from -0.1875 to 0.1875
- w_self: bfloat16 [1024, 1024], replicated, may hold values from -0.1875 to 0.1875
- w_neigh: bfloat16 [1024, 1024], replicated, may hold values from -0.75 to 0.75
- out_gain: bfloat16 [1024], replicated, may hold values from 0.25 to 1.75
- cotangent: bfloat16 [65536, 1024], P(('table', 'dom')), may hold values from -6 to 6
Outputs:
- node_out: bfloat16 [65536, 1024], P(('table', 'dom'))
- table_grad: float32 [8, 131072, 128], P('table', 'dom')
The draws below stay inside these ranges and needn't reach their ends.
Inputs may be any that keep to these rules, and one draw needn't show every extreme that they name: `owner_ids`: the 4 entries of a row differ. Among the 512 rows of one device no owner is named more than 32 times, and in some device's rows some owner is named exactly 32 times. `neighbour_part`: the 4 entries of a row differ. Among the 4 rows of one device no partition is named more than 2 times, and in some device's rows some partition is named exactly 2 times.
All inputs are finite; a program needn't handle non-finite values.
Results may differ from the reference program's by a relative error of at most 0.012.
Values may be sent and summed in bfloat16 or wider, within the bound.
A program may use at most 128 MiB of HBM per device.

```python
import math
import jax
import jax.numpy as jnp
import numpy as np
from jax import lax

E = 128
H = 1024
TOP = 4
FANOUT = 4
BLOCK = 128
NODE_DEV = 512
ROWS_DEV = 8192
NBLK = 4
ROW_CAP = 32
HALO_CAP = 2
NODES = 65536
TABLES = 8
ROWS = 131072
N_DOM = 16
DEVICES = 128


def shuffled_columns(subkey):
    return jax.random.permutation(subkey, BLOCK)


def draw_adjacency(key, part):
    block_total = NODES // BLOCK
    full_shape = (block_total, FANOUT, BLOCK, BLOCK)
    base_key = jax.random.fold_in(key, 11)
    base_level = jnp.exp(jax.random.uniform(base_key, full_shape, jnp.float32, math.log(0.001), math.log(0.01)))
    ranges = ((0.6, 1.0), (0.2, 0.5), (0.0, 0.3))
    column_ids = jnp.arange(BLOCK, dtype=jnp.int32)
    summed = base_level
    for term_index in range(3):
        lower_end, upper_end = ranges[term_index]
        order_key = jax.random.fold_in(key, 101 + term_index)
        weight_key = jax.random.fold_in(key, 201 + term_index)
        order_keys = jax.random.split(order_key, block_total * FANOUT)
        orders = jax.vmap(shuffled_columns)(order_keys).reshape(block_total, FANOUT, BLOCK).astype(jnp.int32)
        weights = jax.random.uniform(weight_key, (block_total, FANOUT, BLOCK), jnp.float32, lower_end, upper_end)
        summed = summed + weights[..., None] * (orders[..., None] == column_ids).astype(jnp.float32)
    return summed.astype(jnp.bfloat16)


def with_ends(values, rng, smallest, high):
    spot = [jax.random.randint(jax.random.fold_in(rng, axis), (), 0, length) for axis, length in enumerate(values.shape)]
    main_axis = values.shape.index(max(values.shape))
    beside = spot[:main_axis] + [(spot[main_axis] + 1) % values.shape[main_axis]] + spot[main_axis + 1:]
    return values.at[tuple(spot)].set(smallest).at[tuple(beside)].set(high)


def levels(rng, extent, pieces, least, top_value):
    factor_of, own = 1.0, jax.random.fold_in(rng, 6)
    for position, blocks in pieces:
        steps = jnp.exp(jax.random.uniform(jax.random.fold_in(own, position), (blocks,), jnp.float32, least / len(pieces), top_value / len(pieces)))
        factor_of = factor_of * jnp.repeat(steps, extent[position] // blocks).reshape([-1 if axis == position else 1 for axis in range(len(extent))])
    return factor_of


def deal_out(stream_key, own, number, rows, amount, top, reach, skew):
    order = jax.random.permutation(stream_key, amount)
    heavy_load, common = portions_of(amount, rows * top, reach, skew, True), portions_of(amount, rows * top, reach, skew, False)
    places = jnp.arange(amount)

    def named(lengths, offset_by):
        used = int((lengths > 0).sum())
        fixed = max(1, used // 4)
        moved = fixed + (places - fixed + offset_by * (used - fixed)) % max(1, amount - fixed)
        return jnp.zeros((amount,), jnp.int32).at[order[jnp.where(places < fixed, places, moved)]].set(jnp.asarray(lengths, jnp.int32))

    lengths = jnp.where(number % 4 == 0, named(heavy_load, number // 4), named(common, number - number // 4 - 1))
    mixed = jax.random.permutation(jax.random.fold_in(own, 3), amount)
    source_of, receiver = mixed[0:amount // 2 * 2:2], mixed[1:amount // 2 * 2:2]
    room = jnp.minimum(lengths[source_of] - 1, reach - lengths[receiver]) // 2
    room = jnp.where((source_of == order[0]) | (receiver == order[0]) | (lengths[receiver] == 0), 0, jnp.maximum(room, 0))
    moved = jax.random.randint(jax.random.fold_in(own, 4), (amount // 2,), 0, 1 << 20) % (room + 1)
    lengths = lengths.at[source_of].add(-moved).at[receiver].add(moved)
    members = jnp.searchsorted(jnp.cumsum(lengths), jnp.arange(rows * top), side="right").astype(jnp.int32)
    table = members.reshape(top, rows).T
    table = table[jax.random.permutation(jax.random.fold_in(own, 1), rows)]
    offset_by = jax.random.randint(jax.random.fold_in(own, 2), (rows, 1), 0, top)
    return jnp.take_along_axis(table, (jnp.arange(top)[None, :] + offset_by) % top, axis=1)


def portions_of(number_of, total, limit, lean, full):
    loads = [(1 << 20) // math.isqrt(grade ** lean) + 1 for grade in range(1, number_of + 1)]
    largest = limit if full else min(limit, max(-(-total // number_of), total * loads[0] // sum(loads)))
    least = 1 if total - largest >= number_of - 1 else 0
    given, rest = [largest] + [least] * (number_of - 1), total - largest - least * (number_of - 1)
    while rest > 0:
        candidates = [i for i in range(1, number_of) if given[i] < largest] or [i for i in range(1, number_of) if given[i] < limit]
        whole, budget = sum([loads[i] for i in candidates]), rest
        for i in candidates:
            addition = min(limit - given[i], max(1, budget * loads[i] // whole), rest)
            given[i] = given[i] + addition
            rest = rest - addition
    return np.array(given)


def bell_draw(rng, shape, width, most, pieces=(), held_as=jnp.bfloat16):
    entries = width * jax.random.normal(rng, shape, jnp.float32)
    if pieces:
        entries = entries * levels(rng, shape, pieces, -0.22, 0.18)
    return jnp.clip(entries, -most, most).astype(held_as)


def setup_inputs(seed: int = 0) -> dict:
    streams_of = jax.random.split(jax.random.key(seed), 13)
    tables = bell_draw(streams_of[0], (TABLES, ROWS, E), 1.0, 6.0, ((0, 8), (1, 16)), jnp.float32)
    owner_ids_keys = jax.random.split(jax.random.fold_in(streams_of[1], 1), NODES // NODE_DEV)
    owner_ids_turns = jax.random.permutation(jax.random.fold_in(streams_of[1], 3), NODES // NODE_DEV)
    owner_ids = jax.vmap(lambda own, number: deal_out(jax.random.fold_in(streams_of[1], 2), own, number, NODE_DEV, DEVICES, TOP, ROW_CAP, 2))(owner_ids_keys, owner_ids_turns).reshape((NODES, TOP))
    row_ids = with_ends(jax.random.randint(streams_of[2], (NODES, TOP), 0, ROWS_DEV), jax.random.fold_in(streams_of[2], 1), 0, ROWS_DEV - 1).astype(jnp.int32)
    neighbour_part_keys = jax.random.split(jax.random.fold_in(streams_of[3], 1), (NODES // BLOCK) // NBLK)
    neighbour_part_turns = jax.random.permutation(jax.random.fold_in(streams_of[3], 3), (NODES // BLOCK) // NBLK)
    neighbour_part = jax.vmap(lambda own, number: deal_out(jax.random.fold_in(streams_of[3], 2), own, number, NBLK, N_DOM, FANOUT, HALO_CAP, 1))(neighbour_part_keys, neighbour_part_turns).reshape((NODES // BLOCK, FANOUT))
    neighbour_block = with_ends(jax.random.randint(streams_of[4], (NODES // BLOCK, FANOUT), 0, NBLK), jax.random.fold_in(streams_of[4], 1), 0, NBLK - 1).astype(jnp.int32)
    adjacency = draw_adjacency(jax.random.fold_in(streams_of[12], 71), 0)
    w_in = bell_draw(streams_of[6], (E, H), E ** -0.5, 0.5)
    w_pool = bell_draw(streams_of[7], (H, H), H ** -0.5, 0.1875)
    w_self = bell_draw(streams_of[8], (H, H), H ** -0.5, 0.1875)
    w_neigh = bell_draw(streams_of[9], (H, H), (H // 16) ** -0.5, 0.75)
    out_gain = jnp.clip(1.0 + 0.15 * jax.random.normal(streams_of[10], (H,), jnp.float32), 0.25, 1.75).astype(jnp.bfloat16)
    cotangent = bell_draw(streams_of[11], (NODES, H), 1.0, 6.0, ((0, 128),))
    return {"tables": tables, "owner_ids": owner_ids, "row_ids": row_ids, "neighbour_part": neighbour_part, "neighbour_block": neighbour_block, "adjacency": adjacency, "w_in": w_in, "w_pool": w_pool, "w_self": w_self, "w_neigh": w_neigh, "out_gain": out_gain, "cotangent": cotangent}


EPSILON = 1e-06

def silu_slope(inputs):
    sigmoid_part = jax.nn.sigmoid(inputs)
    return sigmoid_part * (1.0 + inputs * (1.0 - sigmoid_part))

def rounded(inputs):
    return lax.optimization_barrier(inputs.astype(jnp.bfloat16)).astype(jnp.float32)

def reference(tables, owner_ids, row_ids, neighbour_part, neighbour_block, adjacency, w_in, w_pool, w_self, w_neigh, out_gain, cotangent):
    table_group = (owner_ids // N_DOM).astype(jnp.int32)
    global_rows = (owner_ids % N_DOM * ROWS_DEV + row_ids).astype(jnp.int32)
    looked = tables[table_group, global_rows]
    feature = lax.optimization_barrier(jnp.sum(looked, axis=1))
    hidden = jnp.dot(feature.astype(jnp.bfloat16), w_in, preferred_element_type=jnp.float32).astype(jnp.bfloat16)
    pooled_pre = jnp.dot(hidden, w_pool, preferred_element_type=jnp.float32)
    pooled = jax.nn.silu(pooled_pre).astype(jnp.bfloat16)
    total_blocks = NODES // BLOCK
    group_blocks = N_DOM * NBLK
    home = jnp.arange(total_blocks, dtype=jnp.int32) // group_blocks
    source_index = (home[:, None] * group_blocks + neighbour_part * NBLK + neighbour_block).astype(jnp.int32)
    pooled_blocks = pooled.reshape(total_blocks, BLOCK, H)
    adj_wide = adjacency.astype(jnp.float32)
    inverse = 1.0 / lax.optimization_barrier(jnp.sum(adj_wide, axis=(1, 3)))
    summed = jnp.zeros((total_blocks, BLOCK, H), jnp.float32)
    for column in range(FANOUT):
        picked = pooled_blocks[source_index[:, column]].astype(jnp.float32)
        summed = summed + jnp.einsum('bij,bjh->bih', adj_wide[:, column], picked, precision=lax.Precision.HIGHEST)
    neighbour_mean = (summed * inverse[:, :, None]).astype(jnp.bfloat16).reshape(NODES, H)
    pre_act = jnp.dot(hidden, w_self, preferred_element_type=jnp.float32) + jnp.dot(neighbour_mean, w_neigh, preferred_element_type=jnp.float32)
    active = jax.nn.silu(pre_act)
    rms_scale = lax.rsqrt(lax.optimization_barrier(jnp.mean(active * active, axis=1, keepdims=True)) + EPSILON)
    gain_wide = out_gain.astype(jnp.float32)
    node_out = (active * rms_scale * gain_wide).astype(jnp.bfloat16)
    weighted = gain_wide * cotangent.astype(jnp.float32)
    d_active = rms_scale * weighted - active * (rms_scale * rms_scale * rms_scale) * lax.optimization_barrier(jnp.mean(weighted * active, axis=1, keepdims=True))
    d_pre = (d_active * silu_slope(pre_act)).astype(jnp.bfloat16)
    d_hidden_self = jnp.dot(d_pre, w_self.T, preferred_element_type=jnp.float32)
    d_mean = jnp.dot(d_pre, w_neigh.T, preferred_element_type=jnp.float32)
    d_scaled = rounded(d_mean.reshape(total_blocks, BLOCK, H) * inverse[:, :, None])
    d_pooled = jnp.zeros((total_blocks, BLOCK, H), jnp.float32)
    for column in range(FANOUT):
        share = rounded(jnp.einsum('bij,bih->bjh', adj_wide[:, column], d_scaled, precision=lax.Precision.HIGHEST))
        d_pooled = d_pooled.at[source_index[:, column]].add(share)
    d_pool_pre = (d_pooled.reshape(NODES, H) * silu_slope(pooled_pre)).astype(jnp.bfloat16)
    d_hidden = (d_hidden_self + jnp.dot(d_pool_pre, w_pool.T, preferred_element_type=jnp.float32)).astype(jnp.bfloat16)
    d_feature = jnp.dot(d_hidden, w_in.T, preferred_element_type=jnp.float32)
    spread = jnp.broadcast_to(d_feature[:, None, :], (NODES, TOP, E))
    table_grad = jnp.zeros((TABLES, ROWS, E), jnp.float32).at[table_group, global_rows].add(spread)
    return (node_out, table_grad)
```

```python
import jax
import jax.numpy as jnp
from jax import lax
from jax.experimental import pallas as pl
from jax.experimental.pallas import tpu as pltpu
from jax.sharding import PartitionSpec as P

EPSILON = 1e-06
MESH = pl.DeviceIdType.MESH
F32 = jnp.float32
BF16 = jnp.bfloat16
LIMIT = 60 * 1024 * 1024


def iota(shape, dim):
    return lax.broadcasted_iota(jnp.int32, shape, dim)


def dot(a, b, dims=((1,), (0,))):
    return lax.dot_general(a, b, (dims, ((), ())), preferred_element_type=F32)


def everyone(act):
    table, dom = lax.axis_index("table"), lax.axis_index("dom")
    for step in range(8):
        there = lax.rem(table + step, 8)

        def body(k, carry):
            act(there, lax.rem(dom + k, 16))
            return carry

        lax.fori_loop(0 if step else 1, 16, body, 0)


def greet():
    barrier = pltpu.get_barrier_semaphore()
    everyone(
        lambda t, d: pl.semaphore_signal(barrier, inc=1, device_id=(t, d), device_id_type=MESH)
    )


def met():
    pl.semaphore_wait(pltpu.get_barrier_semaphore(), 127)


def swap_start(out_ref, in_ref, send, recv, local):
    table, dom = lax.axis_index("table"), lax.axis_index("dom")
    me = table * 16 + dom
    pltpu.make_async_copy(out_ref.at[me], in_ref.at[me], local).start()
    everyone(
        lambda t, d: pltpu.make_async_remote_copy(
            out_ref.at[t * 16 + d], in_ref.at[me], send, recv, device_id=(t, d), device_id_type=MESH
        ).start()
    )


def swap_wait(out_ref, in_ref, send, recv, local, others=127):
    table, dom = lax.axis_index("table"), lax.axis_index("dom")
    pltpu.make_async_copy(out_ref.at[0], in_ref.at[0], local).wait()
    whole = pltpu.make_async_remote_copy(
        out_ref.at[pl.ds(0, others)],
        in_ref.at[pl.ds(0, others)],
        send,
        recv,
        device_id=(table, lax.rem(dom + 1, 16)),
        device_id_type=MESH,
    )
    whole.wait_send()
    whole.wait_recv()


def gather_group(fa_ref, send, recv):
    table, dom = lax.axis_index("table"), lax.axis_index("dom")
    z, x = dom // 4, lax.rem(dom, 4)

    def place(h, i, j):
        dz, dx = (j, i) if h == 0 else (i, j)
        return lax.rem(z + dz + 4, 4) * 4 + lax.rem(x + dx + 4, 4)

    def copy(h, number, piece, start, count, to):
        blocks = fa_ref.at[pl.ds(place(h, *piece) * 4 + 2 * h + start, count)]
        return pltpu.make_async_remote_copy(
            blocks,
            blocks,
            send.at[h, number],
            recv.at[h, number],
            device_id=(table, place(h, *to)),
            device_id_type=MESH,
        )

    up, down = (1, 0), (-1, 0)
    away, back = (0, 1), (0, -1)
    pieces = (0, -1, 1, 2)
    first = (up, down)
    across = (away, back)
    sides = (0, 1)

    def near(h, side):
        return copy(h, side, (0, 0), 0, 2, first[side])

    def far(h, side):
        return copy(h, 2 + side, (2 * side - 1, 0), side, 1, first[side])

    def second(h, n, side):
        return copy(h, 4 + 4 * n + side, (pieces[n], 0), 0, 2, across[side])

    def second_far(h, n, side):
        return copy(h, 6 + 4 * n + side, (pieces[n], 2 * side - 1), side, 1, across[side])

    def near_in(h, side):
        return copy(h, side, (2 * side - 1, 0), 0, 2, first[side])

    def far_in(h, side):
        return copy(h, 2 + side, (2, 0), side, 1, first[side])

    def second_in(h, n, side):
        return copy(h, 4 + 4 * n + side, (pieces[n], 2 * side - 1), 0, 2, across[side])

    def second_far_in(h, n, side):
        return copy(h, 6 + 4 * n + side, (pieces[n], 2), side, 1, across[side])

    for h in range(2):
        for side in sides:
            near(h, side).start()
    for h in range(2):
        for side in sides:
            second(h, 0, side).start()
    for side in sides:
        for h in range(2):
            near_in(h, side).wait_recv()
            far(h, side).start()
            for other in sides:
                second(h, 1 + side, other).start()
    for side in sides:
        for h in range(2):
            second_in(h, 0, side).wait_recv()
            second_far(h, 0, side).start()
    for h in range(2):
        for side in sides:
            far_in(h, side).wait_recv()
        for side in sides:
            second(h, 3, side).start()
    for n in (1, 2, 3):
        for side in sides:
            for h in range(2):
                second_in(h, n, side).wait_recv()
                second_far(h, n, side).start()
    for h in range(2):
        for side in sides:
            near(h, side).wait_send()
            far(h, side).wait_send()
            for n in range(4):
                second_far_in(h, n, side).wait_recv()
                second(h, n, side).wait_send()
                second_far(h, n, side).wait_send()


def two_part(w_ref, product):
    high = product.astype(BF16)
    w_ref[0:128, :] = high
    w_ref[128:256, :] = (product - high.astype(F32)).astype(BF16)


def rows_asked(asked):
    above = pltpu.roll(asked, 96, 1)
    row = ((above - 1.0) * 128.0 + asked).astype(jnp.int32)
    low = row >> 10
    return row - low * 1024, low


def front_kernel(
    key_ref,
    key_t_ref,
    tables_ref,
    w_in_ref,
    w_pool_ref,
    w_self_ref,
    fa_ref,
    asked_ref,
    slot_t_ref,
    wip_ref,
    wis_ref,
    table,
    packed,
    request,
    slot,
    wide,
    out_rows,
    in_rows,
    onehot,
    high_b,
    low_b,
    select,
    ordered,
    load_sem,
    swap_sem,
    send,
    recv,
):
    greet()
    load = pltpu.make_async_copy(tables_ref, table, load_sem)
    load.start()
    key, key_t = key_ref[...], key_t_ref[...]
    owner, owner_t = key >> 13, key_t >> 13
    row = key - owner * 8192
    row_a = (row >> 7) + 1
    row_b = row - (row >> 7) * 128
    lanes = iota((512, 128), 1)
    subs = iota((128, 512), 0)
    hits = [jnp.where(owner[:, j : j + 1] == lanes, 1.0, 0.0) for j in range(4)]
    hits_t = [jnp.where(owner_t[j : j + 1, :] == subs, 1.0, 0.0) for j in range(4)]
    hit, hit_t = sum(hits), sum(hits_t)
    lower = jnp.where(iota((512, 512), 0) > iota((512, 512), 1), 1.0, 0.0).astype(BF16)
    upper = jnp.where(iota((512, 512), 0) < iota((512, 512), 1), 1.0, 0.0).astype(BF16)
    rank = dot(lower, hit.astype(BF16))
    rank_t = dot(hit_t.astype(BF16), upper)
    slot[...] = jnp.where(hit > 0.5, rank, -1.0)
    slot_t_ref[...] = jnp.where(hit_t > 0.5, rank_t, -1.0)
    asks = jnp.zeros((128, 128), F32)
    for j in range(4):
        position = jnp.sum(hits[j] * rank, axis=1, keepdims=True).astype(jnp.int32)
        value = jnp.where(lanes == position, row_b[:, j : j + 1].astype(F32), 0.0) + jnp.where(
            lanes == position + 32, row_a[:, j : j + 1].astype(F32), 0.0
        )
        asks = asks + dot(hits_t[j].astype(BF16), value.astype(BF16))
    request[...] = asks.reshape(128, 1, 128)
    met()
    swap_start(request, asked_ref, swap_sem.at[0], swap_sem.at[1], swap_sem.at[2])
    load.wait()
    for c in range(8):
        packed[:, c * 128 : (c + 1) * 128] = table[c * 1024 : (c + 1) * 1024, :].astype(BF16)
    two_part(wip_ref, dot(w_in_ref[...], w_pool_ref[...]))
    two_part(wis_ref, dot(w_in_ref[...], w_self_ref[...]))
    swap_wait(request, asked_ref, swap_sem.at[0], swap_sem.at[1], swap_sem.at[2])

    high, low = rows_asked(asked_ref[...].reshape(128, 128))
    for p in range(32):
        high_b[p] = jnp.broadcast_to(high[:, p : p + 1], (128, 128))
        low_b[p] = jnp.broadcast_to(low[:, p : p + 1], (128, 128))
    lane = iota((128, 128), 1)

    def lookup(g, carry):
        for q in range(8):
            h = high_b[g * 8 + q]
            for c in range(8):
                onehot[q * 128 : (q + 1) * 128, c * 128 : (c + 1) * 128] = jnp.where(
                    h == lane + c * 128, 1.0, 0.0
                ).astype(BF16)
        found = dot(onehot[...], packed[...])
        for q in range(8):
            l = low_b[g * 8 + q]
            total = jnp.zeros((128, 128), F32)
            for c in range(8):
                total = total + jnp.where(
                    l == c, found[q * 128 : (q + 1) * 128, c * 128 : (c + 1) * 128], 0.0
                )
            wide[pl.ds(g * 8 + q, 128, stride=32), :] = total
        return carry

    lax.fori_loop(0, 4, lookup, 0)
    out_rows[...] = wide[...].reshape(128, 32, 128).astype(BF16)
    swap_start(out_rows, in_rows, swap_sem.at[3], swap_sem.at[4], swap_sem.at[5])
    place = slot[...]
    for p in range(32):
        select[:, p * 128 : (p + 1) * 128] = jnp.where(place == float(p), 1.0, 0.0).astype(BF16)
    swap_wait(out_rows, in_rows, swap_sem.at[3], swap_sem.at[4], swap_sem.at[5])
    wide[...] = in_rows[...].astype(F32).reshape(4096, 128)
    for p in range(32):
        ordered[p * 128 : (p + 1) * 128, :] = wide[pl.ds(p, 128, stride=32), :].astype(BF16)
    feature = dot(select[...], ordered[...]).astype(BF16)
    fa_ref[pl.ds(lax.axis_index("dom") * 4, 4)] = feature.reshape(4, 128, 128)
    gather_group(fa_ref, send, recv)


def back_kernel(
    source_ref,
    pair_ref,
    block_ref,
    fa_ref,
    slot_t_ref,
    wip_ref,
    wis_ref,
    w_neigh_ref,
    gain_ref,
    adjacency_ref,
    cotangent_ref,
    node_out_ref,
    in_rows,
    stacked,
    pooled,
    slope,
    inverse,
    mean,
    pre_act,
    d_pre,
    d_scaled,
    d_self,
    parts,
    halo_out,
    halo_in,
    select,
    wide,
    out_rows,
    swap_sem,
):
    table, dom = lax.axis_index("table"), lax.axis_index("dom")
    greet()

    def forward(b, carry):
        for k in range(4):
            f = fa_ref[source_ref[b * 4 + k]]
            stacked[k * 128 : (k + 1) * 128, 0:128] = f
            stacked[k * 128 : (k + 1) * 128, 128:256] = f
        pre = dot(stacked[...], wip_ref[...])
        s = jax.nn.sigmoid(pre)
        pooled[...] = (pre * s).astype(BF16)
        slope[b] = s * (1.0 + pre * (1.0 - s))
        edges = jnp.concatenate([adjacency_ref[b, k] for k in range(4)], axis=1)
        inv = 1.0 / jnp.sum(edges.astype(F32), axis=1, keepdims=True)
        inverse[b] = jnp.broadcast_to(inv, (128, 128))
        mean[b] = (dot(edges, pooled[...]) * inv).astype(BF16)
        return carry

    lax.fori_loop(0, 4, forward, 0)
    own = fa_ref[pl.ds(dom * 4, 4)].reshape(512, 128)
    stacked[:, 0:128] = own
    stacked[:, 128:256] = own
    pre_act[...] = dot(stacked[...], wis_ref[...]) + dot(
        mean[...].reshape(512, 1024), w_neigh_ref[...]
    )
    gain = gain_ref[...].astype(F32)

    def norm(r, carry):
        rows = pl.ds(pl.multiple_of(r * 32, 32), 32)
        pre = pre_act[rows, :]
        s = jax.nn.sigmoid(pre)
        active = pre * s
        rms = lax.rsqrt(jnp.mean(active * active, axis=1, keepdims=True) + EPSILON)
        node_out_ref[rows, :] = (active * rms * gain).astype(BF16)
        weighted = gain * cotangent_ref[rows, :].astype(F32)
        d_active = rms * weighted - active * (rms * rms * rms) * jnp.mean(
            weighted * active, axis=1, keepdims=True
        )
        d_pre[rows, :] = (d_active * (s * (1.0 + pre * (1.0 - s)))).astype(BF16)
        return carry

    lax.fori_loop(0, 16, norm, 0)
    d_mean = dot(d_pre[...], w_neigh_ref[...], ((1,), (1,)))
    for b in range(4):
        d_scaled[b] = (d_mean[b * 128 : (b + 1) * 128, :] * inverse[b][:, 0:1]).astype(BF16)
    both = dot(d_pre[...], wis_ref[...], ((1,), (1,)))
    d_self[...] = (both[:, 0:128] + both[:, 128:256]).reshape(4, 128, 128)

    def backward(b, carry):
        edges = jnp.concatenate([adjacency_ref[b, k].T for k in range(4)], axis=0)
        d_pool = dot(edges, d_scaled[b]) * slope[b]
        pair = dot(d_pool.astype(BF16), wip_ref[...], ((1,), (1,)))
        parts[pl.ds(b * 4, 4)] = (
            (pair[:, 0:128] + pair[:, 128:256]).astype(BF16).reshape(4, 128, 128)
        )
        return carry

    lax.fori_loop(0, 4, backward, 0)
    tag_row = iota((16, 128), 0)

    def fill(q, carry):
        halo_out[q, 0:128, :] = parts[pair_ref[2 * q]]
        halo_out[q, 128:256, :] = parts[pair_ref[2 * q + 1]]
        tag0 = block_ref[2 * q].astype(F32)
        tag1 = block_ref[2 * q + 1].astype(F32)
        halo_out[q, 256:272, :] = jnp.where(tag_row == 0, tag0, tag1).astype(BF16)
        return carry

    lax.fori_loop(0, 16, fill, 0)
    met()
    pltpu.make_async_copy(halo_out.at[dom], halo_in.at[dom], swap_sem.at[2]).start()
    for k in range(1, 16):
        to = lax.rem(dom + k, 16)
        pltpu.make_async_remote_copy(
            halo_out.at[to],
            halo_in.at[dom],
            swap_sem.at[0],
            swap_sem.at[1],
            device_id=(table, to),
            device_id_type=MESH,
        ).start()
    place = slot_t_ref[...]
    for p in range(32):
        select[p * 128 : (p + 1) * 128, :] = jnp.where(place == float(p), 1.0, 0.0).astype(BF16)
    swap_wait(halo_out, halo_in, swap_sem.at[0], swap_sem.at[1], swap_sem.at[2], 15)

    def collect(c, carry):
        total = d_self[c]
        here = c.astype(F32)
        for q in range(16):
            tags = halo_in[q, 256:272, :].astype(F32)
            for s in range(2):
                piece = halo_in[q, s * 128 : (s + 1) * 128, :].astype(F32)
                total = total + jnp.where(tags[s : s + 1, :] == here, piece, 0.0)
        d_self[c] = total
        return carry

    lax.fori_loop(0, 4, collect, 0)
    d_feature = d_self[...].reshape(512, 128).astype(BF16)

    def spread(g, carry):
        rows = dot(select[pl.ds(pl.multiple_of(g * 1024, 1024), 1024), :], d_feature)
        for q in range(8):
            wide[pl.ds(g * 8 + q, 128, stride=32), :] = rows[q * 128 : (q + 1) * 128, :]
        return carry

    lax.fori_loop(0, 4, spread, 0)
    out_rows[...] = wide[...].reshape(128, 32, 128).astype(BF16)
    swap_start(out_rows, in_rows, swap_sem.at[3], swap_sem.at[4], swap_sem.at[5])
    swap_wait(out_rows, in_rows, swap_sem.at[3], swap_sem.at[4], swap_sem.at[5])


def scatter_kernel(asked_ref, rows_ref, grad_ref, low_b, wide, ordered, onehot, terms):
    c2 = pl.program_id(0)

    @pl.when(c2 == 0)
    def _():
        asked = asked_ref[...].reshape(128, 128)
        high, low = rows_asked(asked)
        for p in range(32):
            low_b[p] = jnp.broadcast_to(low[:, p : p + 1], (128, 128))
        high_t = high.T
        for p in range(32):
            onehot[:, p * 128 : (p + 1) * 128] = jnp.where(
                iota((1024, 128), 0) == high_t[p : p + 1, :], 1.0, 0.0
            ).astype(BF16)
        wide[...] = rows_ref[...].astype(F32).reshape(4096, 128)
        for p in range(32):
            ordered[p] = wide[pl.ds(p, 128, stride=32), :]

    for p in range(32):
        for c in range(2):
            terms[p * 128 : (p + 1) * 128, c * 128 : (c + 1) * 128] = jnp.where(
                low_b[p] == c2 * 2 + c, ordered[p], 0.0
            ).astype(BF16)
    total = dot(onehot[...], terms[...])
    grad_ref[0:1024, :] = total[:, 0:128]
    grad_ref[1024:2048, :] = total[:, 128:256]


def whole(count):
    return [pl.BlockSpec(memory_space=pltpu.VMEM)] * count


def body(
    tables,
    owner_ids,
    row_ids,
    neighbour_part,
    neighbour_block,
    adjacency,
    w_in,
    w_pool,
    w_self,
    w_neigh,
    out_gain,
    cotangent,
):
    shape = jax.ShapeDtypeStruct
    vmem = pltpu.VMEM
    key = owner_ids * 8192 + row_ids
    fa, asked, slot_t, wip, wis = pl.pallas_call(
        front_kernel,
        name="front",
        out_shape=(
            shape((64, 128, 128), BF16),
            shape((128, 1, 128), F32),
            shape((128, 512), F32),
            shape((256, 1024), BF16),
            shape((256, 1024), BF16),
        ),
        in_specs=whole(2) + [pl.BlockSpec(memory_space=pl.ANY)] + whole(3),
        out_specs=tuple(whole(5)),
        scratch_shapes=[
            vmem((8192, 128), F32),
            vmem((1024, 1024), BF16),
            vmem((128, 1, 128), F32),
            vmem((512, 128), F32),
            vmem((4096, 128), F32),
            vmem((128, 32, 128), BF16),
            vmem((128, 32, 128), BF16),
            vmem((1024, 1024), BF16),
            vmem((32, 128, 128), jnp.int32),
            vmem((32, 128, 128), jnp.int32),
            vmem((512, 4096), BF16),
            vmem((4096, 128), BF16),
            pltpu.SemaphoreType.DMA,
            pltpu.SemaphoreType.DMA((6,)),
            pltpu.SemaphoreType.DMA((2, 20)),
            pltpu.SemaphoreType.DMA((2, 20)),
        ],
        compiler_params=pltpu.CompilerParams(
            collective_id=0, has_side_effects=True, vmem_limit_bytes=LIMIT
        ),
    )(key, key.T, tables[0], w_in, w_pool, w_self)

    part = neighbour_part.reshape(16)
    block = neighbour_block.reshape(16)
    number = jnp.arange(16, dtype=jnp.int32)
    rank = jnp.sum((part[:, None] == part[None, :]) & (number[None, :] < number[:, None]), axis=1)
    named = (2 * part + rank)[None, :] == jnp.arange(32, dtype=jnp.int32)[:, None]
    pair = jnp.sum(jnp.where(named, number[None, :], 0), axis=1)
    tag = jnp.sum(jnp.where(named, block[None, :] + 1, 0), axis=1) - 1
    node_out, rows = pl.pallas_call(
        back_kernel,
        name="back",
        out_shape=(shape((512, 1024), BF16), shape((128, 32, 128), BF16)),
        in_specs=[pl.BlockSpec(memory_space=pltpu.SMEM)] * 3 + whole(8),
        out_specs=tuple(whole(2)),
        scratch_shapes=[
            vmem((512, 256), BF16),
            vmem((512, 1024), BF16),
            vmem((4, 512, 1024), F32),
            vmem((4, 128, 128), F32),
            vmem((4, 128, 1024), BF16),
            vmem((512, 1024), F32),
            vmem((512, 1024), BF16),
            vmem((4, 128, 1024), BF16),
            vmem((4, 128, 128), F32),
            vmem((16, 128, 128), BF16),
            vmem((16, 272, 128), BF16),
            vmem((16, 272, 128), BF16),
            vmem((4096, 512), BF16),
            vmem((4096, 128), F32),
            vmem((128, 32, 128), BF16),
            pltpu.SemaphoreType.DMA((6,)),
        ],
        compiler_params=pltpu.CompilerParams(
            collective_id=1, has_side_effects=True, vmem_limit_bytes=LIMIT
        ),
    )(
        part * 4 + block,
        pair,
        tag,
        fa,
        slot_t,
        wip,
        wis,
        w_neigh,
        out_gain.reshape(1, 1024),
        adjacency,
        cotangent,
    )
    table_grad = pl.pallas_call(
        scatter_kernel,
        name="scatter",
        grid=(4,),
        out_shape=shape((8192, 128), F32),
        in_specs=whole(2),
        out_specs=pl.BlockSpec((2048, 128), lambda c: (c, 0)),
        scratch_shapes=[
            vmem((32, 128, 128), jnp.int32),
            vmem((4096, 128), F32),
            vmem((32, 128, 128), F32),
            vmem((1024, 4096), BF16),
            vmem((4096, 256), BF16),
        ],
        compiler_params=pltpu.CompilerParams(vmem_limit_bytes=LIMIT),
    )(asked, rows)
    return (node_out, table_grad[None])


def solution(mesh):
    rows = P(("table", "dom"), None)
    placed = (
        P("table", "dom", None),
        rows,
        rows,
        rows,
        rows,
        P(("table", "dom"), None, None, None),
        P(),
        P(),
        P(),
        P(),
        P(),
        rows,
    )
    return jax.shard_map(
        body,
        mesh=mesh,
        in_specs=placed,
        out_specs=(rows, P("table", "dom", None)),
        check_vma=False,
    )
```

```python
import jax
import jax.numpy as jnp
from jax import lax
from jax.experimental import pallas as pl
from jax.experimental.pallas import tpu as pltpu
from jax.sharding import PartitionSpec as P

EPSILON = 1e-06
MESH = pl.DeviceIdType.MESH
F32 = jnp.float32
BF16 = jnp.bfloat16
LIMIT = 62 * 1024 * 1024
NT = ((1,), (1,))


def iota(shape, dim):
    return lax.broadcasted_iota(jnp.int32, shape, dim)


def dot(a, b, dims=((1,), (0,))):
    return lax.dot_general(a, b, (dims, ((), ())), preferred_element_type=F32)


def each_of_table(step, act):
    there = lax.rem(lax.axis_index("table") + step, 8)
    dom = lax.axis_index("dom")

    def body(k, carry):
        act(there, lax.rem(dom + k, 16))
        return carry

    first = jnp.where(step == 0, 1, 0) if not isinstance(step, int) else int(step == 0)
    lax.fori_loop(first, 16, body, 0)


def greet():
    barrier = pltpu.get_barrier_semaphore()
    for step in range(8):
        each_of_table(
            step,
            lambda t, d: pl.semaphore_signal(barrier, inc=1, device_id=(t, d), device_id_type=MESH),
        )


def met():
    pl.semaphore_wait(pltpu.get_barrier_semaphore(), 127)


def send_table(step, out_ref, in_ref, send, recv):
    me = lax.axis_index("table") * 16 + lax.axis_index("dom")
    each_of_table(
        step,
        lambda t, d: pltpu.make_async_remote_copy(
            out_ref.at[t * 16 + d], in_ref.at[me], send, recv, device_id=(t, d), device_id_type=MESH
        ).start(),
    )


def all_of(count, out_ref, in_ref, send, recv):
    return pltpu.make_async_remote_copy(
        out_ref.at[pl.ds(0, count)],
        in_ref.at[pl.ds(0, count)],
        send,
        recv,
        device_id=(lax.axis_index("table"), lax.rem(lax.axis_index("dom") + 1, 16)),
        device_id_type=MESH,
    )


def send_requests(request, asked, send, recv):
    for step in range(8):
        send_table(step, request, asked, send, recv)


def send_halo(halo_out, halo_in, send, recv):
    table, dom = lax.axis_index("table"), lax.axis_index("dom")
    for k in range(1, 16):
        to = lax.rem(dom + k, 16)
        pltpu.make_async_remote_copy(
            halo_out.at[to], halo_in.at[dom], send, recv, device_id=(table, to), device_id_type=MESH
        ).start()


def wait_send(*args):
    all_of(*args).wait_send()


def wait_recv(*args):
    all_of(*args).wait_recv()


def gather_group(fa_ref, send, recv, meanwhile):
    table, dom = lax.axis_index("table"), lax.axis_index("dom")
    z, x = dom // 4, lax.rem(dom, 4)

    def place(h, i, j):
        dz, dx = (j, i) if h == 0 else (i, j)
        return lax.rem(z + dz + 4, 4) * 4 + lax.rem(x + dx + 4, 4)

    def copy(h, number, piece, start, count, to):
        blocks = fa_ref.at[pl.ds(place(h, *piece) * 4 + 2 * h + start, count)]
        return pltpu.make_async_remote_copy(
            blocks,
            blocks,
            send.at[h, number],
            recv.at[h, number],
            device_id=(table, place(h, *to)),
            device_id_type=MESH,
        )

    up, down = (1, 0), (-1, 0)
    away, back = (0, 1), (0, -1)
    pieces = (0, -1, 1, 2)
    first = (up, down)
    across = (away, back)
    sides = (0, 1)

    def near(h, side):
        return copy(h, side, (0, 0), 0, 2, first[side])

    def far(h, side):
        return copy(h, 2 + side, (2 * side - 1, 0), side, 1, first[side])

    def second(h, n, side):
        return copy(h, 4 + 4 * n + side, (pieces[n], 0), 0, 2, across[side])

    def second_far(h, n, side):
        return copy(h, 6 + 4 * n + side, (pieces[n], 2 * side - 1), side, 1, across[side])

    def near_in(h, side):
        return copy(h, side, (2 * side - 1, 0), 0, 2, first[side])

    def far_in(h, side):
        return copy(h, 2 + side, (2, 0), side, 1, first[side])

    def second_in(h, n, side):
        return copy(h, 4 + 4 * n + side, (pieces[n], 2 * side - 1), 0, 2, across[side])

    def second_far_in(h, n, side):
        return copy(h, 6 + 4 * n + side, (pieces[n], 2), side, 1, across[side])

    for h in range(2):
        for side in sides:
            near(h, side).start()
    for h in range(2):
        for side in sides:
            second(h, 0, side).start()
    meanwhile()
    for side in sides:
        for h in range(2):
            near_in(h, side).wait_recv()
            far(h, side).start()
            for other in sides:
                second(h, 1 + side, other).start()
    for side in sides:
        for h in range(2):
            second_in(h, 0, side).wait_recv()
            second_far(h, 0, side).start()
    for h in range(2):
        for side in sides:
            far_in(h, side).wait_recv()
        for side in sides:
            second(h, 3, side).start()
    for n in (1, 2, 3):
        for side in sides:
            for h in range(2):
                second_in(h, n, side).wait_recv()
                second_far(h, n, side).start()
    for h in range(2):
        for side in sides:
            near(h, side).wait_send()
            far(h, side).wait_send()
            for n in range(4):
                second_far_in(h, n, side).wait_recv()
                second(h, n, side).wait_send()
                second_far(h, n, side).wait_send()


def two_part(w_ref, product):
    high = product.astype(BF16)
    w_ref[0:128, :] = high
    w_ref[128:256, :] = (product - high.astype(F32)).astype(BF16)


def step_kernel(
    owner_ref,
    row_ref,
    part_ref,
    block_ref,
    w_in_ref,
    gain_ref,
    tables_hbm,
    w_pool_hbm,
    w_self_hbm,
    w_neigh_hbm,
    adjacency_hbm,
    cotangent_hbm,
    node_out_hbm,
    grad_hbm,
    table,
    w_pool,
    w_self,
    w_neigh,
    adjacency,
    cotangent,
    node_out,
    packed,
    request,
    asked,
    slot,
    row_b,
    out_rows,
    in_rows,
    in_grads,
    onehot,
    select,
    fa,
    wip,
    wis,
    stacked,
    pooled,
    slope,
    inverse,
    mean,
    pre_act,
    d_pre,
    d_scaled,
    d_self,
    parts,
    halo_out,
    halo_in,
    rows_hot,
    terms,
    load_sem,
    one_sem,
    rows_send,
    rows_recv,
    grads_send,
    grads_recv,
    ring_send,
    ring_recv,
    grad_sem,
):
    table_id, dom = lax.axis_index("table"), lax.axis_index("dom")
    me = table_id * 16 + dom
    greet()
    loads = [
        pltpu.make_async_copy(source, target, load_sem.at[i])
        for i, (source, target) in enumerate(
            (
                (tables_hbm, table),
                (w_pool_hbm, w_pool),
                (w_self_hbm, w_self),
                (w_neigh_hbm, w_neigh),
                (adjacency_hbm, adjacency),
                (cotangent_hbm, cotangent),
            )
        )
    ]
    for load in loads:
        load.start()

    subs = iota((128, 512), 0)
    place32 = lax.rem(subs, 32)
    hits = [jnp.where(owner_ref[j : j + 1, :] == subs, 1.0, 0.0) for j in range(4)]
    hit = sum(hits)
    before = jnp.where(iota((512, 512), 0) < iota((512, 512), 1), 1.0, 0.0).astype(BF16)
    rank = dot(hit.astype(BF16), before)
    slot[...] = jnp.where(hit > 0.5, rank, -1.0)
    above = jnp.zeros((128, 128), F32)
    below = jnp.zeros((128, 128), F32)
    for j in range(4):
        position = jnp.sum(hits[j] * rank, axis=0, keepdims=True).astype(jnp.int32)
        row = row_ref[j : j + 1, :]
        row_a = row >> 7
        row_c = (row - row_a * 128).astype(F32)
        row_a = (row_a + 1).astype(F32)
        here = place32 == position
        hot = hits[j].astype(BF16)
        above = above + dot(hot, jnp.where(here, row_a, 0.0).astype(BF16), NT)
        below = below + dot(hot, jnp.where(here, row_c, 0.0).astype(BF16), NT)
    asks = jnp.where(above > 0.5, (above - 1.0) * 128.0 + below, -1.0).astype(jnp.int32)
    request[...] = asks.reshape(128, 1, 128)
    asked[pl.ds(me, 1)] = request[pl.ds(me, 1)]
    met()
    send_requests(request, asked, one_sem.at[0], one_sem.at[1])
    loads[0].wait()
    for c in range(8):
        packed[:, c * 128 : (c + 1) * 128] = table[c * 1024 : (c + 1) * 1024, :].astype(BF16)
    loads[1].wait()
    two_part(wip, dot(w_in_ref[...], w_pool[...]))
    loads[2].wait()
    two_part(wis, dot(w_in_ref[...], w_self[...]))
    wait_recv(127, request, asked, one_sem.at[0], one_sem.at[1])

    asked_t = asked[...].reshape(128, 128).astype(F32).T.astype(jnp.int32)
    for o in range(128):
        row_b[o * 32 : (o + 1) * 32, :] = jnp.broadcast_to(asked_t[0:32, o : o + 1], (32, 128))
    lane = iota((64, 128), 1)

    def lookup(g, carry):
        there = [lax.rem(table_id + 2 * g + i, 8) for i in range(2)]
        for i in range(2):
            for r in range(8):
                start = pl.multiple_of(there[i] * 512 + r * 64, 64)
                high = row_b[pl.ds(start, 64), :] & 1023
                low = i * 512 + r * 64
                for c in range(8):
                    onehot[low : low + 64, c * 128 : (c + 1) * 128] = jnp.where(
                        high == lane + c * 128, 1.0, 0.0
                    ).astype(BF16)
        found = dot(onehot[...], packed[...])
        for i in range(2):
            for r in range(8):
                start = pl.multiple_of(there[i] * 512 + r * 64, 64)
                chunk = row_b[pl.ds(start, 64), :] >> 10
                low = i * 512 + r * 64
                total = jnp.zeros((64, 128), F32)
                for c in range(8):
                    total = total + jnp.where(
                        chunk == c, found[low : low + 64, c * 128 : (c + 1) * 128], 0.0
                    )
                out_rows[pl.ds(there[i] * 16 + r * 2, 2)] = total.astype(BF16).reshape(2, 32, 128)
            send_table(2 * g + i, out_rows, in_rows, rows_send, rows_recv.at[g])
        return carry

    lax.fori_loop(0, 4, lookup, 0)
    in_rows[pl.ds(me, 1)] = out_rows[pl.ds(me, 1)]
    wait_send(127, request, asked, one_sem.at[0], one_sem.at[1])
    sub32 = iota((32, 512), 0).astype(F32)
    for o in range(128):
        select[o * 32 : (o + 1) * 32, :] = jnp.where(slot[o : o + 1, :] == sub32, 1.0, 0.0).astype(
            BF16
        )
    feature_t = jnp.zeros((128, 512), F32)
    for g in range(4):
        wait_recv(31 if g == 0 else 32, out_rows, in_rows, rows_send, rows_recv.at[g])
        for i in range(2):
            there = lax.rem(table_id - 2 * g - i + 8, 8)
            got = in_rows[pl.ds(there * 16, 16)].reshape(512, 128)
            feature_t = feature_t + dot(
                got.T, select[pl.ds(pl.multiple_of(there * 512, 512), 512), :]
            )
    feature = feature_t.T.astype(BF16)
    fa[pl.ds(dom * 4, 4)] = feature.reshape(4, 128, 128)
    stacked[:, 0:128] = feature
    stacked[:, 128:256] = feature

    def meanwhile():
        pre_act[...] = dot(stacked[...], wis[...])
        wait_send(127, out_rows, in_rows, rows_send, rows_recv.at[0])
        for load in loads[3:]:
            load.wait()

    gather_group(fa, ring_send, ring_recv, meanwhile)

    def forward(b, carry):
        for k in range(4):
            f = fa[part_ref[b, k] * 4 + block_ref[b, k]]
            stacked[k * 128 : (k + 1) * 128, 0:128] = f
            stacked[k * 128 : (k + 1) * 128, 128:256] = f
        pre = dot(stacked[...], wip[...])
        s = jax.nn.sigmoid(pre)
        pooled[...] = (pre * s).astype(BF16)
        slope[b] = s * (1.0 + pre * (1.0 - s))
        edges = jnp.concatenate([adjacency[b, k] for k in range(4)], axis=1)
        inv = 1.0 / jnp.sum(edges.astype(F32), axis=1, keepdims=True)
        inverse[b] = jnp.broadcast_to(inv, (128, 128))
        mean[b] = (dot(edges, pooled[...]) * inv).astype(BF16)
        return carry

    lax.fori_loop(0, 4, forward, 0)
    pre_act[...] += dot(mean[...].reshape(512, 1024), w_neigh[...])
    gain = gain_ref[...].astype(F32).reshape(1, 1024)

    def norm(r, carry):
        rows = pl.ds(pl.multiple_of(r * 32, 32), 32)
        pre = pre_act[rows, :]
        s = jax.nn.sigmoid(pre)
        active = pre * s
        rms = lax.rsqrt(jnp.mean(active * active, axis=1, keepdims=True) + EPSILON)
        node_out[rows, :] = (active * rms * gain).astype(BF16)
        weighted = gain * cotangent[rows, :].astype(F32)
        d_active = rms * weighted - active * (rms * rms * rms) * jnp.mean(
            weighted * active, axis=1, keepdims=True
        )
        d_pre[rows, :] = (d_active * (s * (1.0 + pre * (1.0 - s)))).astype(BF16)
        return carry

    lax.fori_loop(0, 16, norm, 0)
    store = pltpu.make_async_copy(node_out, node_out_hbm, load_sem.at[6])
    store.start()
    d_mean = dot(d_pre[...], w_neigh[...], NT)
    for b in range(4):
        d_scaled[b] = (d_mean[b * 128 : (b + 1) * 128, :] * inverse[b][:, 0:1]).astype(BF16)
    both = dot(d_pre[...], wis[...], NT)
    d_self[...] = (both[:, 0:128] + both[:, 128:256]).reshape(4, 128, 128)

    def backward(b, carry):
        edges = jnp.concatenate([adjacency[b, k].T for k in range(4)], axis=0)
        d_pool = dot(edges, d_scaled[b]) * slope[b]
        pair = dot(d_pool.astype(BF16), wip[...], NT)
        parts[pl.ds(b * 4, 4)] = (
            (pair[:, 0:128] + pair[:, 128:256]).astype(BF16).reshape(4, 128, 128)
        )
        return carry

    lax.fori_loop(0, 4, backward, 0)
    tag_row = iota((16, 128), 0)

    def fill(q, carry):
        count = jnp.int32(0)
        pairs = [jnp.int32(0), jnp.int32(0)]
        tags = [jnp.int32(-1), jnp.int32(-1)]
        for i in range(16):
            named = part_ref[i // 4, i % 4] == q
            for s in range(2):
                taken = named & (count == s)
                pairs[s] = jnp.where(taken, i, pairs[s])
                tags[s] = jnp.where(taken, block_ref[i // 4, i % 4], tags[s])
            count = count + jnp.where(named, 1, 0)
        halo_out[q, 0:128, :] = parts[pairs[0]]
        halo_out[q, 128:256, :] = parts[pairs[1]]
        halo_out[q, 256:272, :] = jnp.where(
            tag_row == 0, tags[0].astype(F32), tags[1].astype(F32)
        ).astype(BF16)
        return carry

    lax.fori_loop(0, 16, fill, 0)
    halo_in[pl.ds(dom, 1)] = halo_out[pl.ds(dom, 1)]
    send_halo(halo_out, halo_in, one_sem.at[2], one_sem.at[3])
    lane4 = iota((1, 128), 1) >> 5
    tall = iota((1024, 128), 0)

    def heat(t, carry):
        names = asked[pl.ds(t * 16, 16)].reshape(16, 128) & 1023
        for i in range(4):
            mixed = names[4 * i : 4 * i + 1, :]
            for k in range(1, 4):
                mixed = jnp.where(lane4 == k, names[4 * i + k : 4 * i + k + 1, :], mixed)
            rows_hot[t, :, i * 128 : (i + 1) * 128] = jnp.where(tall == mixed, 1.0, 0.0).astype(
                BF16
            )
        return carry

    lax.fori_loop(0, 8, heat, 0)
    wait_recv(15, halo_out, halo_in, one_sem.at[2], one_sem.at[3])

    def collect(c, carry):
        total = d_self[c]
        here = c.astype(F32)
        for q in range(16):
            tags = halo_in[q, 256:272, :].astype(F32)
            for s in range(2):
                piece = halo_in[q, s * 128 : (s + 1) * 128, :].astype(F32)
                total = total + jnp.where(tags[s : s + 1, :] == here, piece, 0.0)
        d_self[c] = total
        return carry

    lax.fori_loop(0, 4, collect, 0)
    d_feature = d_self[...].reshape(512, 128).astype(BF16)

    def spread(step, carry):
        there = lax.rem(table_id + step, 8)
        rows = dot(select[pl.ds(pl.multiple_of(there * 512, 512), 512), :], d_feature)
        out_rows[pl.ds(there * 16, 16)] = rows.astype(BF16).reshape(16, 32, 128)
        send_table(step, out_rows, in_grads, grads_send, grads_recv.at[step // 2])
        return carry

    lax.fori_loop(0, 8, spread, 0)
    in_grads[pl.ds(me, 1)] = out_rows[pl.ds(me, 1)]
    wait_send(15, halo_out, halo_in, one_sem.at[2], one_sem.at[3])

    for g in range(4):
        wait_recv(31 if g == 0 else 32, out_rows, in_grads, grads_send, grads_recv.at[g])
        there = [lax.rem(table_id - 2 * g - i + 8, 8) for i in range(2)]
        for i in range(2):
            onehot[:, i * 512 : (i + 1) * 512] = rows_hot[there[i]]

        def add(c2, carry):
            for i in range(2):
                for r in range(8):
                    start = pl.multiple_of(there[i] * 512 + r * 64, 64)
                    chunk = row_b[pl.ds(start, 64), :] >> 10
                    low = i * 512 + r * 64
                    rows = (
                        in_grads[pl.ds(there[i] * 16 + r * 2, 2)].reshape(64, 128).astype(F32)
                    )
                    for c in range(2):
                        terms[low : low + 64, c * 128 : (c + 1) * 128] = jnp.where(
                            chunk == c2 * 2 + c, rows, 0.0
                        ).astype(BF16)
            total = dot(onehot[...], terms[...])
            for c in range(2):
                rows = pl.ds(pl.multiple_of((c2 * 2 + c) * 1024, 1024), 1024)
                if g == 0:
                    table[rows, :] = total[:, c * 128 : (c + 1) * 128]
                else:
                    table[rows, :] += total[:, c * 128 : (c + 1) * 128]
            if g == 3:
                rows = pl.ds(pl.multiple_of(c2 * 2048, 2048), 2048)
                pltpu.make_async_copy(table.at[rows], grad_hbm.at[rows], grad_sem.at[c2]).start()
            return carry

        lax.fori_loop(0, 4, add, 0)
    wait_send(127, out_rows, in_grads, grads_send, grads_recv.at[0])
    store.wait()
    for c2 in range(4):
        rows = pl.ds(c2 * 2048, 2048)
        pltpu.make_async_copy(table.at[rows], grad_hbm.at[rows], grad_sem.at[c2]).wait()


def body(
    tables,
    owner_ids,
    row_ids,
    neighbour_part,
    neighbour_block,
    adjacency,
    w_in,
    w_pool,
    w_self,
    w_neigh,
    out_gain,
    cotangent,
):
    shape = jax.ShapeDtypeStruct
    vmem = pltpu.VMEM
    dma = pltpu.SemaphoreType.DMA
    held = [pl.BlockSpec(memory_space=pltpu.VMEM)]
    scalar = [pl.BlockSpec(memory_space=pltpu.SMEM)]
    anywhere = [pl.BlockSpec(memory_space=pl.ANY)]
    node_out, table_grad = pl.pallas_call(
        step_kernel,
        name="step",
        out_shape=(shape((512, 1024), BF16), shape((8192, 128), F32)),
        in_specs=held * 2 + scalar * 2 + held * 2 + anywhere * 6,
        out_specs=tuple(anywhere * 2),
        scratch_shapes=[
            vmem((8192, 128), F32),
            vmem((1024, 1024), BF16),
            vmem((1024, 1024), BF16),
            vmem((1024, 1024), BF16),
            vmem((4, 4, 128, 128), BF16),
            vmem((512, 1024), BF16),
            vmem((512, 1024), BF16),
            vmem((1024, 1024), BF16),
            vmem((128, 1, 128), jnp.int32),
            vmem((128, 1, 128), jnp.int32),
            vmem((128, 512), F32),
            vmem((4096, 128), jnp.int32),
            vmem((128, 32, 128), BF16),
            vmem((128, 32, 128), BF16),
            vmem((128, 32, 128), BF16),
            vmem((1024, 1024), BF16),
            vmem((4096, 512), BF16),
            vmem((64, 128, 128), BF16),
            vmem((256, 1024), BF16),
            vmem((256, 1024), BF16),
            vmem((512, 256), BF16),
            vmem((512, 1024), BF16),
            vmem((4, 512, 1024), F32),
            vmem((4, 128, 128), F32),
            vmem((4, 128, 1024), BF16),
            vmem((512, 1024), F32),
            vmem((512, 1024), BF16),
            vmem((4, 128, 1024), BF16),
            vmem((4, 128, 128), F32),
            vmem((16, 128, 128), BF16),
            vmem((16, 272, 128), BF16),
            vmem((16, 272, 128), BF16),
            vmem((8, 1024, 512), BF16),
            vmem((1024, 256), BF16),
            dma((7,)),
            dma((4,)),
            dma,
            dma((4,)),
            dma,
            dma((4,)),
            dma((2, 20)),
            dma((2, 20)),
            dma((4,)),
        ],
        compiler_params=pltpu.CompilerParams(
            collective_id=0, has_side_effects=True, vmem_limit_bytes=LIMIT
        ),
    )(
        owner_ids.T,
        row_ids.T,
        neighbour_part,
        neighbour_block,
        w_in,
        out_gain,
        tables[0],
        w_pool,
        w_self,
        w_neigh,
        adjacency,
        cotangent,
    )
    return (node_out, table_grad[None])


def solution(mesh):
    rows = P(("table", "dom"), None)
    placed = (
        P("table", "dom", None),
        rows,
        rows,
        rows,
        rows,
        P(("table", "dom"), None, None, None),
        P(),
        P(),
        P(),
        P(),
        P(),
        rows,
    )
    return jax.shard_map(
        body,
        mesh=mesh,
        in_specs=placed,
        out_specs=(rows, P("table", "dom", None)),
        check_vma=False,
    )
```

```python
import jax
import jax.numpy as jnp
from jax import lax
from jax.experimental import pallas as pl
from jax.experimental.pallas import tpu as pltpu
from jax.sharding import PartitionSpec as P

EPSILON = 1e-06
MESH = pl.DeviceIdType.MESH
F32 = jnp.float32
BF16 = jnp.bfloat16
LIMIT = 62 * 1024 * 1024
NT = ((1,), (1,))


def iota(shape, dim):
    return lax.broadcasted_iota(jnp.int32, shape, dim)


def dot(a, b, dims=((1,), (0,))):
    return lax.dot_general(a, b, (dims, ((), ())), preferred_element_type=F32)


def each_of_table(step, act):
    there = lax.rem(lax.axis_index("table") + step, 8)
    dom = lax.axis_index("dom")

    def body(k, carry):
        act(there, lax.rem(dom + k, 16))
        return carry

    first = jnp.where(step == 0, 1, 0) if not isinstance(step, int) else int(step == 0)
    lax.fori_loop(first, 16, body, 0)


def peers():
    table, dom = lax.axis_index("table"), lax.axis_index("dom")
    return [(lax.rem(table + k, 8), dom) for k in range(1, 8)] + [
        (table, lax.rem(dom + k, 16)) for k in range(1, 16)
    ]


def greet():
    barrier = pltpu.get_barrier_semaphore()
    for peer in peers():
        pl.semaphore_signal(barrier, inc=1, device_id=peer, device_id_type=MESH)


def met():
    pl.semaphore_wait(pltpu.get_barrier_semaphore(), 22)


def send_table(step, out_ref, in_ref, send, recv):
    me = lax.axis_index("table") * 16 + lax.axis_index("dom")
    each_of_table(
        step,
        lambda t, d: pltpu.make_async_remote_copy(
            out_ref.at[t * 16 + d], in_ref.at[me], send, recv, device_id=(t, d), device_id_type=MESH
        ).start(),
    )


def all_of(count, out_ref, in_ref, send, recv):
    return pltpu.make_async_remote_copy(
        out_ref.at[pl.ds(0, count)],
        in_ref.at[pl.ds(0, count)],
        send,
        recv,
        device_id=(lax.axis_index("table"), lax.rem(lax.axis_index("dom") + 1, 16)),
        device_id_type=MESH,
    )


def ask_tables(request, relay, send, recv):
    table = lax.axis_index("table")
    for peer in peers()[:7]:
        pltpu.make_async_remote_copy(
            request.at[peer[0]], relay.at[table], send, recv, device_id=peer, device_id_type=MESH
        ).start()


def ask_group(relay, asked, send, recv):
    dom = lax.axis_index("dom")
    for peer in peers()[7:]:
        pltpu.make_async_remote_copy(
            relay.at[:, peer[1]], asked.at[:, dom], send, recv, device_id=peer, device_id_type=MESH
        ).start()


def wait_tables(request, relay, send, recv):
    whole = pltpu.make_async_remote_copy(
        request.at[pl.ds(0, 7)],
        relay.at[pl.ds(0, 7)],
        send,
        recv,
        device_id=peers()[0],
        device_id_type=MESH,
    )
    whole.wait_recv()
    whole.wait_send()


def asked_group(relay, asked, send, recv):
    return pltpu.make_async_remote_copy(
        relay.at[:, pl.ds(0, 15)],
        asked.at[:, pl.ds(0, 15)],
        send,
        recv,
        device_id=peers()[7],
        device_id_type=MESH,
    )


def wait_group(*args):
    asked_group(*args).wait_recv()


def sent_group(*args):
    asked_group(*args).wait_send()


def pairs_of(part_ref, block_ref, q):
    count = jnp.int32(0)
    pairs = [jnp.int32(0), jnp.int32(0)]
    tags = [jnp.int32(-1), jnp.int32(-1)]
    for i in range(16):
        named = part_ref[i // 4, i % 4] == q
        for s in range(2):
            taken = named & (count == s)
            pairs[s] = jnp.where(taken, i, pairs[s])
            tags[s] = jnp.where(taken, block_ref[i // 4, i % 4], tags[s])
        count = count + jnp.where(named, 1, 0)
    return pairs, tags


def send_halo(halo_out, halo_in, send, recv):
    table, dom = lax.axis_index("table"), lax.axis_index("dom")
    for k in range(1, 16):
        to = lax.rem(dom + k, 16)
        pltpu.make_async_remote_copy(
            halo_out.at[to], halo_in.at[dom], send, recv, device_id=(table, to), device_id_type=MESH
        ).start()


def wait_send(*args):
    all_of(*args).wait_send()


def wait_recv(*args):
    all_of(*args).wait_recv()


def gather_group(fa_ref, send, recv, meanwhile):
    table, dom = lax.axis_index("table"), lax.axis_index("dom")
    z, x = dom // 4, lax.rem(dom, 4)

    def place(h, i, j):
        dz, dx = (j, i) if h == 0 else (i, j)
        return lax.rem(z + dz + 4, 4) * 4 + lax.rem(x + dx + 4, 4)

    def copy(h, number, piece, start, count, to):
        blocks = fa_ref.at[pl.ds(place(h, *piece) * 4 + 2 * h + start, count)]
        return pltpu.make_async_remote_copy(
            blocks,
            blocks,
            send.at[h, number],
            recv.at[h, number],
            device_id=(table, place(h, *to)),
            device_id_type=MESH,
        )

    up, down = (1, 0), (-1, 0)
    away, back = (0, 1), (0, -1)
    pieces = (0, -1, 1, 2)
    first = (up, down)
    across = (away, back)
    sides = (0, 1)

    def near(h, side):
        return copy(h, side, (0, 0), 0, 2, first[side])

    def far(h, side):
        return copy(h, 2 + side, (2 * side - 1, 0), side, 1, first[side])

    def second(h, n, side):
        return copy(h, 4 + 4 * n + side, (pieces[n], 0), 0, 2, across[side])

    def second_far(h, n, side):
        return copy(h, 6 + 4 * n + side, (pieces[n], 2 * side - 1), side, 1, across[side])

    def near_in(h, side):
        return copy(h, side, (2 * side - 1, 0), 0, 2, first[side])

    def far_in(h, side):
        return copy(h, 2 + side, (2, 0), side, 1, first[side])

    def second_in(h, n, side):
        return copy(h, 4 + 4 * n + side, (pieces[n], 2 * side - 1), 0, 2, across[side])

    def second_far_in(h, n, side):
        return copy(h, 6 + 4 * n + side, (pieces[n], 2), side, 1, across[side])

    for h in range(2):
        for side in sides:
            near(h, side).start()
    for h in range(2):
        for side in sides:
            second(h, 0, side).start()
    meanwhile()
    for side in sides:
        for h in range(2):
            near_in(h, side).wait_recv()
            far(h, side).start()
            for other in sides:
                second(h, 1 + side, other).start()
    for side in sides:
        for h in range(2):
            second_in(h, 0, side).wait_recv()
            second_far(h, 0, side).start()
    for h in range(2):
        for side in sides:
            far_in(h, side).wait_recv()
        for side in sides:
            second(h, 3, side).start()
    for n in (1, 2, 3):
        for side in sides:
            for h in range(2):
                second_in(h, n, side).wait_recv()
                second_far(h, n, side).start()
    for h in range(2):
        for side in sides:
            near(h, side).wait_send()
            far(h, side).wait_send()
            for n in range(4):
                second_far_in(h, n, side).wait_recv()
                second(h, n, side).wait_send()
                second_far(h, n, side).wait_send()


def two_part(w_ref, product):
    high = product.astype(BF16)
    w_ref[0:128, :] = high
    w_ref[128:256, :] = (product - high.astype(F32)).astype(BF16)


def step_kernel(
    owner_ref,
    row_ref,
    part_ref,
    block_ref,
    w_in_ref,
    gain_ref,
    tables_hbm,
    w_pool_hbm,
    w_self_hbm,
    w_neigh_hbm,
    adjacency_hbm,
    cotangent_hbm,
    node_out_hbm,
    sums_hbm,
    hot_hbm,
    low_hbm,
    late_hbm,
    table,
    w_pool,
    w_self,
    w_neigh,
    adjacency,
    cotangent,
    node_out,
    packed,
    request,
    relay,
    asked,
    slot,
    row_b,
    out_rows,
    in_rows,
    in_grads,
    onehot,
    select,
    fa,
    wip,
    wis,
    stacked,
    pooled,
    slope,
    inverse,
    mean,
    pre_act,
    d_pre,
    d_scaled,
    d_self,
    parts,
    halo_out,
    halo_in,
    rows_hot,
    terms,
    load_sem,
    one_sem,
    rows_send,
    rows_recv,
    grads_send,
    grads_recv,
    ring_send,
    ring_recv,
    grad_sem,
):
    table_id, dom = lax.axis_index("table"), lax.axis_index("dom")
    me = table_id * 16 + dom
    greet()
    loads = [
        pltpu.make_async_copy(source, target, load_sem.at[i])
        for i, (source, target) in enumerate(
            (
                (tables_hbm, table),
                (w_pool_hbm, w_pool),
                (w_self_hbm, w_self),
                (w_neigh_hbm, w_neigh),
                (adjacency_hbm, adjacency),
                (cotangent_hbm, cotangent),
            )
        )
    ]
    for load in loads:
        load.start()

    subs = iota((128, 512), 0)
    place32 = lax.rem(subs, 32)
    hits = [jnp.where(owner_ref[j : j + 1, :] == subs, 1.0, 0.0) for j in range(4)]
    hit = sum(hits)
    before = jnp.where(iota((512, 512), 0) < iota((512, 512), 1), 1.0, 0.0).astype(BF16)
    rank = dot(hit.astype(BF16), before)
    slot[...] = jnp.where(hit > 0.5, rank, -1.0)
    above = jnp.zeros((128, 128), F32)
    below = jnp.zeros((128, 128), F32)
    for j in range(4):
        position = jnp.sum(hits[j] * rank, axis=0, keepdims=True).astype(jnp.int32)
        row = row_ref[j : j + 1, :]
        row_a = row >> 7
        row_c = (row - row_a * 128).astype(F32)
        row_a = (row_a + 1).astype(F32)
        here = place32 == position
        hot = hits[j].astype(BF16)
        above = above + dot(hot, jnp.where(here, row_a, 0.0).astype(BF16), NT)
        below = below + dot(hot, jnp.where(here, row_c, 0.0).astype(BF16), NT)
    asks = jnp.where(above > 0.5, (above - 1.0) * 128.0 + below, -1.0).astype(jnp.int32)
    request[...] = asks.reshape(8, 16, 1, 128)
    relay[pl.ds(table_id, 1)] = request[pl.ds(table_id, 1)]

    def tag(q, carry):
        _, tags = pairs_of(part_ref, block_ref, q)
        for s in range(2):
            relay[8 + s, q] = jnp.full((1, 128), tags[s], jnp.int32)
        return carry

    lax.fori_loop(0, 16, tag, 0)
    met()
    ask_tables(request, relay, one_sem.at[0], one_sem.at[1])
    loads[0].wait()
    for c in range(8):
        packed[:, c * 128 : (c + 1) * 128] = table[c * 1024 : (c + 1) * 1024, :].astype(BF16)
    wait_tables(request, relay, one_sem.at[0], one_sem.at[1])
    asked[:, pl.ds(dom, 1)] = relay[:, pl.ds(dom, 1)]
    ask_group(relay, asked, one_sem.at[4], one_sem.at[5])
    loads[1].wait()
    two_part(wip, dot(w_in_ref[...], w_pool[...]))
    loads[2].wait()
    two_part(wis, dot(w_in_ref[...], w_self[...]))
    wait_group(relay, asked, one_sem.at[4], one_sem.at[5])

    asked_t = asked[0:8].reshape(128, 128).astype(F32).T.astype(jnp.int32)
    for o in range(128):
        row_b[o * 32 : (o + 1) * 32, :] = jnp.broadcast_to(asked_t[0:32, o : o + 1], (32, 128))
    lane = iota((64, 128), 1)

    def lookup(g, carry):
        there = [lax.rem(table_id + 2 * g + i, 8) for i in range(2)]
        for i in range(2):
            for r in range(8):
                start = pl.multiple_of(there[i] * 512 + r * 64, 64)
                high = row_b[pl.ds(start, 64), :] & 1023
                low = i * 512 + r * 64
                for c in range(8):
                    onehot[low : low + 64, c * 128 : (c + 1) * 128] = jnp.where(
                        high == lane + c * 128, 1.0, 0.0
                    ).astype(BF16)
        found = dot(onehot[...], packed[...])
        for i in range(2):
            for r in range(8):
                start = pl.multiple_of(there[i] * 512 + r * 64, 64)
                chunk = row_b[pl.ds(start, 64), :] >> 10
                low = i * 512 + r * 64
                total = jnp.zeros((64, 128), F32)
                for c in range(8):
                    total = total + jnp.where(
                        chunk == c, found[low : low + 64, c * 128 : (c + 1) * 128], 0.0
                    )
                out_rows[pl.ds(there[i] * 16 + r * 2, 2)] = total.astype(BF16).reshape(2, 32, 128)
            send_table(2 * g + i, out_rows, in_rows, rows_send, rows_recv.at[g])
        return carry

    lax.fori_loop(0, 4, lookup, 0)
    in_rows[pl.ds(me, 1)] = out_rows[pl.ds(me, 1)]
    sent_group(relay, asked, one_sem.at[4], one_sem.at[5])
    sub32 = iota((32, 512), 0).astype(F32)
    for o in range(128):
        select[o * 32 : (o + 1) * 32, :] = jnp.where(slot[o : o + 1, :] == sub32, 1.0, 0.0).astype(
            BF16
        )
    feature_t = jnp.zeros((128, 512), F32)
    for g in range(4):
        wait_recv(31 if g == 0 else 32, out_rows, in_rows, rows_send, rows_recv.at[g])
        for i in range(2):
            there = lax.rem(table_id - 2 * g - i + 8, 8)
            got = in_rows[pl.ds(there * 16, 16)].reshape(512, 128)
            feature_t = feature_t + dot(
                got.T, select[pl.ds(pl.multiple_of(there * 512, 512), 512), :]
            )
    feature = feature_t.T.astype(BF16)
    fa[pl.ds(dom * 4, 4)] = feature.reshape(4, 128, 128)
    stacked[:, 0:128] = feature
    stacked[:, 128:256] = feature

    def meanwhile():
        pre_act[...] = dot(stacked[...], wis[...])
        wait_send(127, out_rows, in_rows, rows_send, rows_recv.at[0])
        for load in loads[3:]:
            load.wait()

    gather_group(fa, ring_send, ring_recv, meanwhile)

    def forward(b, carry):
        for k in range(4):
            f = fa[part_ref[b, k] * 4 + block_ref[b, k]]
            stacked[k * 128 : (k + 1) * 128, 0:128] = f
            stacked[k * 128 : (k + 1) * 128, 128:256] = f
        pre = dot(stacked[...], wip[...])
        s = jax.nn.sigmoid(pre)
        pooled[...] = (pre * s).astype(BF16)
        slope[b] = s * (1.0 + pre * (1.0 - s))
        edges = jnp.concatenate([adjacency[b, k] for k in range(4)], axis=1)
        inv = 1.0 / jnp.sum(edges.astype(F32), axis=1, keepdims=True)
        inverse[b] = jnp.broadcast_to(inv, (128, 128))
        mean[b] = (dot(edges, pooled[...]) * inv).astype(BF16)
        return carry

    lax.fori_loop(0, 4, forward, 0)
    pre_act[...] += dot(mean[...].reshape(512, 1024), w_neigh[...])
    gain = gain_ref[...].astype(F32).reshape(1, 1024)

    def norm(r, carry):
        rows = pl.ds(pl.multiple_of(r * 32, 32), 32)
        pre = pre_act[rows, :]
        s = jax.nn.sigmoid(pre)
        active = pre * s
        rms = lax.rsqrt(jnp.mean(active * active, axis=1, keepdims=True) + EPSILON)
        node_out[rows, :] = (active * rms * gain).astype(BF16)
        weighted = gain * cotangent[rows, :].astype(F32)
        d_active = rms * weighted - active * (rms * rms * rms) * jnp.mean(
            weighted * active, axis=1, keepdims=True
        )
        d_pre[rows, :] = (d_active * (s * (1.0 + pre * (1.0 - s)))).astype(BF16)
        return carry

    lax.fori_loop(0, 16, norm, 0)
    store = pltpu.make_async_copy(node_out, node_out_hbm, load_sem.at[6])
    store.start()
    d_mean = dot(d_pre[...], w_neigh[...], NT)
    for b in range(4):
        d_scaled[b] = (d_mean[b * 128 : (b + 1) * 128, :] * inverse[b][:, 0:1]).astype(BF16)

    for half in range(2):
        first = half * 64

        def backward(b, carry):
            edges = jnp.concatenate(
                [adjacency[b, k].T[first : first + 64] for k in range(4)], axis=0
            )
            slopes = jnp.concatenate(
                [slope[b, k * 128 + first : k * 128 + first + 64, :] for k in range(4)], axis=0
            )
            d_pool = dot(edges, d_scaled[b]) * slopes
            pair = dot(d_pool.astype(BF16), wip[...], NT)
            parts[pl.ds(b * 4, 4)] = (
                (pair[:, 0:128] + pair[:, 128:256]).astype(BF16).reshape(4, 64, 128)
            )
            return carry

        lax.fori_loop(0, 4, backward, 0)

        def fill(q, carry):
            pairs, _ = pairs_of(part_ref, block_ref, q)
            for s in range(2):
                halo_out[half, q, s] = parts[pairs[s]]
            return carry

        lax.fori_loop(0, 16, fill, 0)
        halo_in[half, pl.ds(dom, 1)] = halo_out[half, pl.ds(dom, 1)]
        send_halo(
            halo_out.at[half], halo_in.at[half], one_sem.at[2 + 4 * half], one_sem.at[3 + 4 * half]
        )
    lane4 = iota((1, 128), 1) >> 5
    tall = iota((1024, 128), 0)

    def heat(g, carry):
        for i in range(2):
            there = lax.rem(table_id - 2 * g - i + 8, 8)
            names = asked[there].reshape(16, 128) & 1023
            for n in range(4):
                mixed = names[4 * n : 4 * n + 1, :]
                for k in range(1, 4):
                    mixed = jnp.where(lane4 == k, names[4 * n + k : 4 * n + k + 1, :], mixed)
                low = i * 512 + n * 128
                rows_hot[g, :, low : low + 128] = jnp.where(tall == mixed, 1.0, 0.0).astype(BF16)
        return carry

    lax.fori_loop(0, 4, heat, 0)
    last = [lax.rem(table_id - 6 - i + 8, 8) for i in range(2)]
    saves = [pltpu.make_async_copy(rows_hot.at[3], hot_hbm, grad_sem.at[0])] + [
        pltpu.make_async_copy(
            row_b.at[pl.ds(pl.multiple_of(last[i] * 512, 512), 512)],
            low_hbm.at[pl.ds(i * 512, 512)],
            grad_sem.at[1 + i],
        )
        for i in range(2)
    ]
    for save in saves:
        save.start()
    both = dot(d_pre[...], wis[...], NT)
    d_self[...] = (both[:, 0:128] + both[:, 128:256]).reshape(4, 128, 128)
    for half in range(2):
        wait_recv(
            15,
            halo_out.at[half],
            halo_in.at[half],
            one_sem.at[2 + 4 * half],
            one_sem.at[3 + 4 * half],
        )
        rows = slice(half * 64, half * 64 + 64)

        def collect(c, carry):
            total = d_self[c, rows, :]
            for q in range(16):
                for s in range(2):
                    total = total + jnp.where(
                        asked[8 + s, q] == c, halo_in[half, q, s].astype(F32), 0.0
                    )
            d_self[c, rows, :] = total
            return carry

        lax.fori_loop(0, 4, collect, 0)
    d_feature = d_self[...].reshape(512, 128).astype(BF16)

    def spread(step, carry):
        there = lax.rem(table_id + step, 8)
        rows = dot(select[pl.ds(pl.multiple_of(there * 512, 512), 512), :], d_feature)
        out_rows[pl.ds(there * 16, 16)] = rows.astype(BF16).reshape(16, 32, 128)
        send_table(step, out_rows, in_grads, grads_send, grads_recv.at[step // 2])
        return carry

    lax.fori_loop(0, 8, spread, 0)
    in_grads[pl.ds(me, 1)] = out_rows[pl.ds(me, 1)]
    for half in range(2):
        wait_send(
            15,
            halo_out.at[half],
            halo_in.at[half],
            one_sem.at[2 + 4 * half],
            one_sem.at[3 + 4 * half],
        )

    for g in range(3):
        wait_recv(31 if g == 0 else 32, out_rows, in_grads, grads_send, grads_recv.at[g])
        for i in range(2):
            there = lax.rem(table_id - 2 * g - i + 8, 8)
            for r in range(8):
                start = pl.multiple_of(there * 512 + r * 64, 64)
                chunk = row_b[pl.ds(start, 64), :] >> 10
                rows = in_grads[pl.ds(there * 16 + r * 2, 2)].reshape(64, 128).astype(F32)
                low = i * 512 + r * 64
                for c in range(8):
                    terms[low : low + 64, c * 128 : (c + 1) * 128] = jnp.where(
                        chunk == c, rows, 0.0
                    ).astype(BF16)
        for c2 in range(4):
            total = dot(rows_hot[g], terms[:, c2 * 256 : (c2 + 1) * 256])
            for c in range(2):
                start = (c2 * 2 + c) * 1024
                if g == 0:
                    table[start : start + 1024, :] = total[:, c * 128 : (c + 1) * 128]
                else:
                    table[start : start + 1024, :] += total[:, c * 128 : (c + 1) * 128]
    saves.append(pltpu.make_async_copy(table, sums_hbm, grad_sem.at[3]))
    saves[-1].start()
    wait_recv(32, out_rows, in_grads, grads_send, grads_recv.at[3])
    for i in range(2):
        saves.append(
            pltpu.make_async_copy(
                in_grads.at[pl.ds(last[i] * 16, 16)],
                late_hbm.at[pl.ds(i * 16, 16)],
                grad_sem.at[4 + i],
            )
        )
        saves[-1].start()
    wait_send(127, out_rows, in_grads, grads_send, grads_recv.at[0])
    store.wait()
    for save in saves:
        save.wait()


def last_kernel(hot, row_b, late, sums, node, grad, node_out, terms):
    c2 = pl.program_id(0)
    node_out[...] = node[...]
    for r in range(16):
        chunk = row_b[r * 64 : (r + 1) * 64, :] >> 10
        rows = late[2 * r : 2 * r + 2].reshape(64, 128).astype(F32)
        for c in range(2):
            terms[r * 64 : (r + 1) * 64, c * 128 : (c + 1) * 128] = jnp.where(
                chunk == c2 * 2 + c, rows, 0.0
            ).astype(BF16)
    total = dot(hot[...], terms[...])
    for c in range(2):
        part = slice(c * 1024, (c + 1) * 1024)
        grad[part, :] = sums[part, :] + total[:, c * 128 : (c + 1) * 128]


def body(
    tables,
    owner_ids,
    row_ids,
    neighbour_part,
    neighbour_block,
    adjacency,
    w_in,
    w_pool,
    w_self,
    w_neigh,
    out_gain,
    cotangent,
):
    shape = jax.ShapeDtypeStruct
    vmem = pltpu.VMEM
    dma = pltpu.SemaphoreType.DMA
    held = [pl.BlockSpec(memory_space=pltpu.VMEM)]
    scalar = [pl.BlockSpec(memory_space=pltpu.SMEM)]
    anywhere = [pl.BlockSpec(memory_space=pl.ANY)]
    node, sums, hot, low, late = pl.pallas_call(
        step_kernel,
        name="step",
        out_shape=(
            shape((512, 1024), BF16),
            shape((8192, 128), F32),
            shape((1024, 1024), BF16),
            shape((1024, 128), jnp.int32),
            shape((32, 32, 128), BF16),
        ),
        in_specs=held * 2 + scalar * 2 + held * 2 + anywhere * 6,
        out_specs=tuple(anywhere * 5),
        scratch_shapes=[
            vmem((8192, 128), F32),
            vmem((1024, 1024), BF16),
            vmem((1024, 1024), BF16),
            vmem((1024, 1024), BF16),
            vmem((4, 4, 128, 128), BF16),
            vmem((512, 1024), BF16),
            vmem((512, 1024), BF16),
            vmem((1024, 1024), BF16),
            vmem((8, 16, 1, 128), jnp.int32),
            vmem((10, 16, 1, 128), jnp.int32),
            vmem((10, 16, 1, 128), jnp.int32),
            vmem((128, 512), F32),
            vmem((4096, 128), jnp.int32),
            vmem((128, 32, 128), BF16),
            vmem((128, 32, 128), BF16),
            vmem((128, 32, 128), BF16),
            vmem((1024, 1024), BF16),
            vmem((4096, 512), BF16),
            vmem((64, 128, 128), BF16),
            vmem((256, 1024), BF16),
            vmem((256, 1024), BF16),
            vmem((512, 256), BF16),
            vmem((512, 1024), BF16),
            vmem((4, 512, 1024), F32),
            vmem((4, 128, 128), F32),
            vmem((4, 128, 1024), BF16),
            vmem((512, 1024), F32),
            vmem((512, 1024), BF16),
            vmem((4, 128, 1024), BF16),
            vmem((4, 128, 128), F32),
            vmem((16, 64, 128), BF16),
            vmem((2, 16, 2, 64, 128), BF16),
            vmem((2, 16, 2, 64, 128), BF16),
            vmem((4, 1024, 1024), BF16),
            vmem((1024, 1024), BF16),
            dma((7,)),
            dma((8,)),
            dma,
            dma((4,)),
            dma,
            dma((4,)),
            dma((2, 20)),
            dma((2, 20)),
            dma((6,)),
        ],
        compiler_params=pltpu.CompilerParams(
            collective_id=0, has_side_effects=True, vmem_limit_bytes=LIMIT
        ),
    )(
        owner_ids.T,
        row_ids.T,
        neighbour_part,
        neighbour_block,
        w_in,
        out_gain,
        tables[0],
        w_pool,
        w_self,
        w_neigh,
        adjacency,
        cotangent,
    )
    table_grad, node_out = pl.pallas_call(
        last_kernel,
        name="last",
        grid=(4,),
        out_shape=(shape((8192, 128), F32), shape((512, 1024), BF16)),
        in_specs=held * 3
        + [
            pl.BlockSpec((2048, 128), lambda c: (c, 0)),
            pl.BlockSpec((128, 1024), lambda c: (c, 0)),
        ],
        out_specs=(
            pl.BlockSpec((2048, 128), lambda c: (c, 0)),
            pl.BlockSpec((128, 1024), lambda c: (c, 0)),
        ),
        scratch_shapes=[vmem((1024, 256), BF16)],
        compiler_params=pltpu.CompilerParams(vmem_limit_bytes=LIMIT),
    )(hot, low, late, sums, node)
    return (node_out, table_grad[None])


def solution(mesh):
    rows = P(("table", "dom"), None)
    placed = (
        P("table", "dom", None),
        rows,
        rows,
        rows,
        rows,
        P(("table", "dom"), None, None, None),
        P(),
        P(),
        P(),
        P(),
        P(),
        rows,
    )
    return jax.shard_map(
        body,
        mesh=mesh,
        in_specs=placed,
        out_specs=(rows, P("table", "dom", None)),
        check_vma=False,
    )
```

```python
import jax
import jax.numpy as jnp
from jax import lax
from jax.experimental import pallas as pl
from jax.experimental.pallas import tpu as pltpu
from jax.sharding import PartitionSpec as P

EPSILON = 1e-06
MESH = pl.DeviceIdType.MESH
F32 = jnp.float32
BF16 = jnp.bfloat16
LIMIT = 62 * 1024 * 1024
NT = ((1,), (1,))


def iota(shape, dim):
    return lax.broadcasted_iota(jnp.int32, shape, dim)


def dot(a, b, dims=((1,), (0,))):
    return lax.dot_general(a, b, (dims, ((), ())), preferred_element_type=F32)


def each_of_table(step, act):
    there = lax.rem(lax.axis_index("table") + step, 8)
    dom = lax.axis_index("dom")

    def body(k, carry):
        act(there, lax.rem(dom + k, 16))
        return carry

    first = jnp.where(step == 0, 1, 0) if not isinstance(step, int) else int(step == 0)
    lax.fori_loop(first, 16, body, 0)


def peers():
    table, dom = lax.axis_index("table"), lax.axis_index("dom")
    return [(lax.rem(table + k, 8), dom) for k in range(1, 8)] + [
        (table, lax.rem(dom + k, 16)) for k in range(1, 16)
    ]


def greet():
    barrier = pltpu.get_barrier_semaphore()
    for peer in peers():
        pl.semaphore_signal(barrier, inc=1, device_id=peer, device_id_type=MESH)


def met():
    pl.semaphore_wait(pltpu.get_barrier_semaphore(), 22)


def send_table(step, out_ref, in_ref, send, recv):
    me = lax.axis_index("table") * 16 + lax.axis_index("dom")
    each_of_table(
        step,
        lambda t, d: pltpu.make_async_remote_copy(
            out_ref.at[t * 16 + d], in_ref.at[me], send, recv, device_id=(t, d), device_id_type=MESH
        ).start(),
    )


def all_of(count, out_ref, in_ref, send, recv):
    return pltpu.make_async_remote_copy(
        out_ref.at[pl.ds(0, count)],
        in_ref.at[pl.ds(0, count)],
        send,
        recv,
        device_id=(lax.axis_index("table"), lax.rem(lax.axis_index("dom") + 1, 16)),
        device_id_type=MESH,
    )


def ask_tables(request, relay, send, recv):
    table = lax.axis_index("table")
    for peer in peers()[:7]:
        pltpu.make_async_remote_copy(
            request.at[peer[0]], relay.at[table], send, recv, device_id=peer, device_id_type=MESH
        ).start()


def ask_group(relay, asked, send, recv):
    dom = lax.axis_index("dom")
    for peer in peers()[7:]:
        pltpu.make_async_remote_copy(
            relay.at[:, peer[1]], asked.at[:, dom], send, recv, device_id=peer, device_id_type=MESH
        ).start()


def wait_tables(request, relay, send, recv):
    whole = pltpu.make_async_remote_copy(
        request.at[pl.ds(0, 7)],
        relay.at[pl.ds(0, 7)],
        send,
        recv,
        device_id=peers()[0],
        device_id_type=MESH,
    )
    whole.wait_recv()
    whole.wait_send()


def asked_group(relay, asked, send, recv):
    return pltpu.make_async_remote_copy(
        relay.at[:, pl.ds(0, 15)],
        asked.at[:, pl.ds(0, 15)],
        send,
        recv,
        device_id=peers()[7],
        device_id_type=MESH,
    )


def wait_group(*args):
    asked_group(*args).wait_recv()


def sent_group(*args):
    asked_group(*args).wait_send()


def pairs_of(part_ref, block_ref, q):
    count = jnp.int32(0)
    pairs = [jnp.int32(0), jnp.int32(0)]
    tags = [jnp.int32(-1), jnp.int32(-1)]
    for i in range(16):
        named = part_ref[i // 4, i % 4] == q
        for s in range(2):
            taken = named & (count == s)
            pairs[s] = jnp.where(taken, i, pairs[s])
            tags[s] = jnp.where(taken, block_ref[i // 4, i % 4], tags[s])
        count = count + jnp.where(named, 1, 0)
    return pairs, tags


def send_halo(halo_out, halo_in, send, recv):
    table, dom = lax.axis_index("table"), lax.axis_index("dom")
    for k in range(1, 16):
        to = lax.rem(dom + k, 16)
        pltpu.make_async_remote_copy(
            halo_out.at[to], halo_in.at[dom], send, recv, device_id=(table, to), device_id_type=MESH
        ).start()


def wait_send(*args):
    all_of(*args).wait_send()


def wait_recv(*args):
    all_of(*args).wait_recv()


def gather_group(fa_ref, send, recv, meanwhile):
    table, dom = lax.axis_index("table"), lax.axis_index("dom")
    z, x = dom // 4, lax.rem(dom, 4)

    def place(h, i, j):
        dz, dx = (j, i) if h == 0 else (i, j)
        return lax.rem(z + dz + 4, 4) * 4 + lax.rem(x + dx + 4, 4)

    def copy(h, number, piece, start, count, to):
        blocks = fa_ref.at[pl.ds(place(h, *piece) * 4 + 2 * h + start, count)]
        return pltpu.make_async_remote_copy(
            blocks,
            blocks,
            send.at[h, number],
            recv.at[h, number],
            device_id=(table, place(h, *to)),
            device_id_type=MESH,
        )

    up, down = (1, 0), (-1, 0)
    away, back = (0, 1), (0, -1)
    pieces = (0, -1, 1, 2)
    first = (up, down)
    across = (away, back)
    sides = (0, 1)

    def near(h, side):
        return copy(h, side, (0, 0), 0, 2, first[side])

    def far(h, side):
        return copy(h, 2 + side, (2 * side - 1, 0), side, 1, first[side])

    def second(h, n, side):
        return copy(h, 4 + 4 * n + side, (pieces[n], 0), 0, 2, across[side])

    def second_far(h, n, side):
        return copy(h, 6 + 4 * n + side, (pieces[n], 2 * side - 1), side, 1, across[side])

    def near_in(h, side):
        return copy(h, side, (2 * side - 1, 0), 0, 2, first[side])

    def far_in(h, side):
        return copy(h, 2 + side, (2, 0), side, 1, first[side])

    def second_in(h, n, side):
        return copy(h, 4 + 4 * n + side, (pieces[n], 2 * side - 1), 0, 2, across[side])

    def second_far_in(h, n, side):
        return copy(h, 6 + 4 * n + side, (pieces[n], 2), side, 1, across[side])

    for h in range(2):
        for side in sides:
            near(h, side).start()
    for h in range(2):
        for side in sides:
            second(h, 0, side).start()
    meanwhile()
    for side in sides:
        for h in range(2):
            near_in(h, side).wait_recv()
            far(h, side).start()
            for other in sides:
                second(h, 1 + side, other).start()
    for side in sides:
        for h in range(2):
            second_in(h, 0, side).wait_recv()
            second_far(h, 0, side).start()
    for h in range(2):
        for side in sides:
            far_in(h, side).wait_recv()
        for side in sides:
            second(h, 3, side).start()
    for n in (1, 2, 3):
        for side in sides:
            for h in range(2):
                second_in(h, n, side).wait_recv()
                second_far(h, n, side).start()
    for h in range(2):
        for side in sides:
            near(h, side).wait_send()
            far(h, side).wait_send()
            for n in range(4):
                second_far_in(h, n, side).wait_recv()
                second(h, n, side).wait_send()
                second_far(h, n, side).wait_send()


def two_part(w_ref, product):
    high = product.astype(BF16)
    w_ref[0:128, :] = high
    w_ref[128:256, :] = (product - high.astype(F32)).astype(BF16)


def step_kernel(
    owner_ref,
    row_ref,
    part_ref,
    block_ref,
    w_in_ref,
    gain_ref,
    tables_hbm,
    w_pool_hbm,
    w_self_hbm,
    w_neigh_hbm,
    adjacency_hbm,
    cotangent_hbm,
    node_out_hbm,
    sums_hbm,
    hot_hbm,
    low_hbm,
    late_hbm,
    table,
    w_pool,
    w_self,
    w_neigh,
    adjacency,
    cotangent,
    node_out,
    packed,
    request,
    relay,
    asked,
    slot,
    row_b,
    out_rows,
    in_rows,
    in_grads,
    onehot,
    select,
    fa,
    wip,
    wis,
    stacked,
    pooled,
    slope,
    inverse,
    mean,
    pre_act,
    d_pre,
    d_scaled,
    d_self,
    parts,
    halo_out,
    halo_in,
    rows_hot,
    terms,
    load_sem,
    one_sem,
    rows_send,
    rows_recv,
    grads_send,
    grads_recv,
    ring_send,
    ring_recv,
    grad_sem,
):
    table_id, dom = lax.axis_index("table"), lax.axis_index("dom")
    me = table_id * 16 + dom
    greet()
    loads = [
        pltpu.make_async_copy(source, target, load_sem.at[i])
        for i, (source, target) in enumerate(
            (
                (tables_hbm, table),
                (w_pool_hbm, w_pool),
                (w_self_hbm, w_self),
                (w_neigh_hbm, w_neigh),
                (adjacency_hbm, adjacency),
                (cotangent_hbm, cotangent),
            )
        )
    ]
    for load in loads:
        load.start()

    subs = iota((128, 512), 0)
    place32 = lax.rem(subs, 32)
    hits = [jnp.where(owner_ref[j : j + 1, :] == subs, 1.0, 0.0) for j in range(4)]
    hit = sum(hits)
    before = jnp.where(iota((512, 512), 0) < iota((512, 512), 1), 1.0, 0.0).astype(BF16)
    rank = dot(hit.astype(BF16), before)
    slot[...] = jnp.where(hit > 0.5, rank, -1.0)
    above = jnp.zeros((128, 128), F32)
    below = jnp.zeros((128, 128), F32)
    for j in range(4):
        position = jnp.sum(hits[j] * rank, axis=0, keepdims=True).astype(jnp.int32)
        row = row_ref[j : j + 1, :]
        row_a = row >> 7
        row_c = (row - row_a * 128).astype(F32)
        row_a = (row_a + 1).astype(F32)
        here = place32 == position
        hot = hits[j].astype(BF16)
        above = above + dot(hot, jnp.where(here, row_a, 0.0).astype(BF16), NT)
        below = below + dot(hot, jnp.where(here, row_c, 0.0).astype(BF16), NT)
    asks = jnp.where(above > 0.5, (above - 1.0) * 128.0 + below, -1.0).astype(jnp.int32)
    request[...] = asks.reshape(8, 16, 1, 128)
    relay[pl.ds(table_id, 1)] = request[pl.ds(table_id, 1)]

    def tag(q, carry):
        _, tags = pairs_of(part_ref, block_ref, q)
        for s in range(2):
            relay[8 + s, q] = jnp.full((1, 128), tags[s], jnp.int32)
        return carry

    lax.fori_loop(0, 16, tag, 0)
    met()
    ask_tables(request, relay, one_sem.at[0], one_sem.at[1])
    loads[0].wait()
    for c in range(8):
        packed[:, c * 128 : (c + 1) * 128] = table[c * 1024 : (c + 1) * 1024, :].astype(BF16)
    wait_tables(request, relay, one_sem.at[0], one_sem.at[1])
    asked[:, pl.ds(dom, 1)] = relay[:, pl.ds(dom, 1)]
    ask_group(relay, asked, one_sem.at[4], one_sem.at[5])
    loads[1].wait()
    two_part(wip, dot(w_in_ref[...], w_pool[...]))
    loads[2].wait()
    two_part(wis, dot(w_in_ref[...], w_self[...]))
    wait_group(relay, asked, one_sem.at[4], one_sem.at[5])

    asked_t = asked[0:8].reshape(128, 128).astype(F32).T.astype(jnp.int32)
    for o in range(128):
        row_b[o * 32 : (o + 1) * 32, :] = jnp.broadcast_to(asked_t[0:32, o : o + 1], (32, 128))
    lane = iota((64, 128), 1)

    def lookup(g, carry):
        there = [lax.rem(table_id + 2 * g + i, 8) for i in range(2)]
        for i in range(2):
            for r in range(8):
                start = pl.multiple_of(there[i] * 512 + r * 64, 64)
                high = row_b[pl.ds(start, 64), :] & 1023
                low = i * 512 + r * 64
                for c in range(8):
                    onehot[low : low + 64, c * 128 : (c + 1) * 128] = jnp.where(
                        high == lane + c * 128, 1.0, 0.0
                    ).astype(BF16)
        found = dot(onehot[...], packed[...])
        for i in range(2):
            for r in range(8):
                start = pl.multiple_of(there[i] * 512 + r * 64, 64)
                chunk = row_b[pl.ds(start, 64), :] >> 10
                low = i * 512 + r * 64
                total = jnp.zeros((64, 128), F32)
                for c in range(8):
                    total = total + jnp.where(
                        chunk == c, found[low : low + 64, c * 128 : (c + 1) * 128], 0.0
                    )
                out_rows[pl.ds(there[i] * 16 + r * 2, 2)] = total.astype(BF16).reshape(2, 32, 128)
            send_table(2 * g + i, out_rows, in_rows, rows_send, rows_recv.at[g])
        return carry

    lax.fori_loop(0, 4, lookup, 0)
    in_rows[pl.ds(me, 1)] = out_rows[pl.ds(me, 1)]
    sent_group(relay, asked, one_sem.at[4], one_sem.at[5])
    sub32 = iota((32, 512), 0).astype(F32)
    for o in range(128):
        select[o * 32 : (o + 1) * 32, :] = jnp.where(slot[o : o + 1, :] == sub32, 1.0, 0.0).astype(
            BF16
        )
    feature_t = jnp.zeros((128, 512), F32)
    for g in range(4):
        wait_recv(31 if g == 0 else 32, out_rows, in_rows, rows_send, rows_recv.at[g])
        for i in range(2):
            there = lax.rem(table_id - 2 * g - i + 8, 8)
            got = in_rows[pl.ds(there * 16, 16)].reshape(512, 128)
            feature_t = feature_t + dot(
                got.T, select[pl.ds(pl.multiple_of(there * 512, 512), 512), :]
            )
    feature = feature_t.T.astype(BF16)
    fa[pl.ds(dom * 4, 4)] = feature.reshape(4, 128, 128)
    stacked[:, 0:128] = feature
    stacked[:, 128:256] = feature

    def meanwhile():
        pre_act[...] = dot(stacked[...], wis[...])
        wait_send(127, out_rows, in_rows, rows_send, rows_recv.at[0])
        for load in loads[3:]:
            load.wait()

    gather_group(fa, ring_send, ring_recv, meanwhile)

    def forward(b, carry):
        for k in range(4):
            f = fa[part_ref[b, k] * 4 + block_ref[b, k]]
            stacked[k * 128 : (k + 1) * 128, 0:128] = f
            stacked[k * 128 : (k + 1) * 128, 128:256] = f
        pre = dot(stacked[...], wip[...])
        s = jax.nn.sigmoid(pre)
        pooled[...] = (pre * s).astype(BF16)
        slope[b] = s * (1.0 + pre * (1.0 - s))
        edges = jnp.concatenate([adjacency[b, k] for k in range(4)], axis=1)
        inv = 1.0 / jnp.sum(edges.astype(F32), axis=1, keepdims=True)
        inverse[b] = jnp.broadcast_to(inv, (128, 128))
        mean[b] = (dot(edges, pooled[...]) * inv).astype(BF16)
        return carry

    lax.fori_loop(0, 4, forward, 0)
    pre_act[...] += dot(mean[...].reshape(512, 1024), w_neigh[...])
    gain = gain_ref[...].astype(F32).reshape(1, 1024)

    def norm(r, carry):
        rows = pl.ds(pl.multiple_of(r * 64, 64), 64)
        pre = pre_act[rows, :]
        s = jax.nn.sigmoid(pre)
        active = pre * s
        rms = lax.rsqrt(jnp.mean(active * active, axis=1, keepdims=True) + EPSILON)
        node_out[rows, :] = (active * rms * gain).astype(BF16)
        weighted = gain * cotangent[rows, :].astype(F32)
        d_active = rms * weighted - active * (rms * rms * rms) * jnp.mean(
            weighted * active, axis=1, keepdims=True
        )
        d_pre[rows, :] = (d_active * (s * (1.0 + pre * (1.0 - s)))).astype(BF16)
        return carry

    lax.fori_loop(0, 8, norm, 0)
    store = pltpu.make_async_copy(node_out, node_out_hbm, load_sem.at[6])
    store.start()
    d_mean = dot(d_pre[...], w_neigh[...], NT)
    for b in range(4):
        d_scaled[b] = (d_mean[b * 128 : (b + 1) * 128, :] * inverse[b][:, 0:1]).astype(BF16)

    for half in range(2):
        first = half * 64

        def backward(b, carry):
            edges = jnp.concatenate(
                [adjacency[b, k].T[first : first + 64] for k in range(4)], axis=0
            )
            slopes = jnp.concatenate(
                [slope[b, k * 128 + first : k * 128 + first + 64, :] for k in range(4)], axis=0
            )
            d_pool = dot(edges, d_scaled[b]) * slopes
            pair = dot(d_pool.astype(BF16), wip[...], NT)
            parts[pl.ds(b * 4, 4)] = (
                (pair[:, 0:128] + pair[:, 128:256]).astype(BF16).reshape(4, 64, 128)
            )
            return carry

        lax.fori_loop(0, 4, backward, 0)

        def fill(q, carry):
            pairs, _ = pairs_of(part_ref, block_ref, q)
            for s in range(2):
                halo_out[half, q, s] = parts[pairs[s]]
            return carry

        lax.fori_loop(0, 16, fill, 0)
        halo_in[half, pl.ds(dom, 1)] = halo_out[half, pl.ds(dom, 1)]
        send_halo(
            halo_out.at[half], halo_in.at[half], one_sem.at[2 + 4 * half], one_sem.at[3 + 4 * half]
        )
    lane4 = iota((1, 128), 1) >> 5
    tall = iota((1024, 128), 0)

    def heat(g, carry):
        for i in range(2):
            there = lax.rem(table_id - 2 * g - i + 8, 8)
            names = asked[there].reshape(16, 128) & 1023
            for n in range(4):
                mixed = names[4 * n : 4 * n + 1, :]
                for k in range(1, 4):
                    mixed = jnp.where(lane4 == k, names[4 * n + k : 4 * n + k + 1, :], mixed)
                low = i * 512 + n * 128
                rows_hot[g, :, low : low + 128] = jnp.where(tall == mixed, 1.0, 0.0).astype(BF16)
        return carry

    lax.fori_loop(0, 4, heat, 0)
    last = [lax.rem(table_id - 6 - i + 8, 8) for i in range(2)]
    saves = [pltpu.make_async_copy(rows_hot.at[3], hot_hbm, grad_sem.at[0])] + [
        pltpu.make_async_copy(
            row_b.at[pl.ds(pl.multiple_of(last[i] * 512, 512), 512)],
            low_hbm.at[pl.ds(i * 512, 512)],
            grad_sem.at[1 + i],
        )
        for i in range(2)
    ]
    for save in saves:
        save.start()
    both = dot(d_pre[...], wis[...], NT)
    d_self[...] = (both[:, 0:128] + both[:, 128:256]).reshape(4, 128, 128)
    for half in range(2):
        wait_recv(
            15,
            halo_out.at[half],
            halo_in.at[half],
            one_sem.at[2 + 4 * half],
            one_sem.at[3 + 4 * half],
        )
        rows = slice(half * 64, half * 64 + 64)

        def collect(c, carry):
            total = d_self[c, rows, :]
            for q in range(16):
                for s in range(2):
                    total = total + jnp.where(
                        asked[8 + s, q] == c, halo_in[half, q, s].astype(F32), 0.0
                    )
            d_self[c, rows, :] = total
            return carry

        lax.fori_loop(0, 4, collect, 0)
    d_feature = d_self[...].reshape(512, 128).astype(BF16)

    def spread(step, carry):
        there = lax.rem(table_id + step, 8)
        rows = dot(select[pl.ds(pl.multiple_of(there * 512, 512), 512), :], d_feature)
        out_rows[pl.ds(there * 16, 16)] = rows.astype(BF16).reshape(16, 32, 128)
        send_table(step, out_rows, in_grads, grads_send, grads_recv.at[step // 2])
        return carry

    lax.fori_loop(0, 8, spread, 0)
    in_grads[pl.ds(me, 1)] = out_rows[pl.ds(me, 1)]
    for half in range(2):
        wait_send(
            15,
            halo_out.at[half],
            halo_in.at[half],
            one_sem.at[2 + 4 * half],
            one_sem.at[3 + 4 * half],
        )

    for g in range(3):
        wait_recv(31 if g == 0 else 32, out_rows, in_grads, grads_send, grads_recv.at[g])
        for i in range(2):
            there = lax.rem(table_id - 2 * g - i + 8, 8)
            for r in range(8):
                start = pl.multiple_of(there * 512 + r * 64, 64)
                chunk = row_b[pl.ds(start, 64), :] >> 10
                rows = in_grads[pl.ds(there * 16 + r * 2, 2)].reshape(64, 128).astype(F32)
                low = i * 512 + r * 64
                for c in range(8):
                    terms[low : low + 64, c * 128 : (c + 1) * 128] = jnp.where(
                        chunk == c, rows, 0.0
                    ).astype(BF16)
        for c2 in range(4):
            total = dot(rows_hot[g], terms[:, c2 * 256 : (c2 + 1) * 256])
            for c in range(2):
                start = (c2 * 2 + c) * 1024
                if g == 0:
                    table[start : start + 1024, :] = total[:, c * 128 : (c + 1) * 128]
                else:
                    table[start : start + 1024, :] += total[:, c * 128 : (c + 1) * 128]
    saves.append(pltpu.make_async_copy(table, sums_hbm, grad_sem.at[3]))
    saves[-1].start()
    wait_recv(32, out_rows, in_grads, grads_send, grads_recv.at[3])
    for i in range(2):
        saves.append(
            pltpu.make_async_copy(
                in_grads.at[pl.ds(last[i] * 16, 16)],
                late_hbm.at[pl.ds(i * 16, 16)],
                grad_sem.at[4 + i],
            )
        )
        saves[-1].start()
    wait_send(127, out_rows, in_grads, grads_send, grads_recv.at[0])
    store.wait()
    for save in saves:
        save.wait()


def last_kernel(hot, row_b, late, sums, node, grad, node_out, terms):
    c2 = pl.program_id(0)
    node_out[...] = node[...]
    for r in range(16):
        chunk = row_b[r * 64 : (r + 1) * 64, :] >> 10
        rows = late[2 * r : 2 * r + 2].reshape(64, 128).astype(F32)
        for c in range(2):
            terms[r * 64 : (r + 1) * 64, c * 128 : (c + 1) * 128] = jnp.where(
                chunk == c2 * 2 + c, rows, 0.0
            ).astype(BF16)
    total = dot(hot[...], terms[...])
    for c in range(2):
        part = slice(c * 1024, (c + 1) * 1024)
        grad[part, :] = sums[part, :] + total[:, c * 128 : (c + 1) * 128]


def body(
    tables,
    owner_ids,
    row_ids,
    neighbour_part,
    neighbour_block,
    adjacency,
    w_in,
    w_pool,
    w_self,
    w_neigh,
    out_gain,
    cotangent,
):
    shape = jax.ShapeDtypeStruct
    vmem = pltpu.VMEM
    dma = pltpu.SemaphoreType.DMA
    held = [pl.BlockSpec(memory_space=pltpu.VMEM)]
    scalar = [pl.BlockSpec(memory_space=pltpu.SMEM)]
    anywhere = [pl.BlockSpec(memory_space=pl.ANY)]
    node, sums, hot, low, late = pl.pallas_call(
        step_kernel,
        name="step",
        out_shape=(
            shape((512, 1024), BF16),
            shape((8192, 128), F32),
            shape((1024, 1024), BF16),
            shape((1024, 128), jnp.int32),
            shape((32, 32, 128), BF16),
        ),
        in_specs=held * 2 + scalar * 2 + held * 2 + anywhere * 6,
        out_specs=tuple(anywhere * 5),
        scratch_shapes=[
            vmem((8192, 128), F32),
            vmem((1024, 1024), BF16),
            vmem((1024, 1024), BF16),
            vmem((1024, 1024), BF16),
            vmem((4, 4, 128, 128), BF16),
            vmem((512, 1024), BF16),
            vmem((512, 1024), BF16),
            vmem((1024, 1024), BF16),
            vmem((8, 16, 1, 128), jnp.int32),
            vmem((10, 16, 1, 128), jnp.int32),
            vmem((10, 16, 1, 128), jnp.int32),
            vmem((128, 512), F32),
            vmem((4096, 128), jnp.int32),
            vmem((128, 32, 128), BF16),
            vmem((128, 32, 128), BF16),
            vmem((128, 32, 128), BF16),
            vmem((1024, 1024), BF16),
            vmem((4096, 512), BF16),
            vmem((64, 128, 128), BF16),
            vmem((256, 1024), BF16),
            vmem((256, 1024), BF16),
            vmem((512, 256), BF16),
            vmem((512, 1024), BF16),
            vmem((4, 512, 1024), F32),
            vmem((4, 128, 128), F32),
            vmem((4, 128, 1024), BF16),
            vmem((512, 1024), F32),
            vmem((512, 1024), BF16),
            vmem((4, 128, 1024), BF16),
            vmem((4, 128, 128), F32),
            vmem((16, 64, 128), BF16),
            vmem((2, 16, 2, 64, 128), BF16),
            vmem((2, 16, 2, 64, 128), BF16),
            vmem((4, 1024, 1024), BF16),
            vmem((1024, 1024), BF16),
            dma((7,)),
            dma((8,)),
            dma,
            dma((4,)),
            dma,
            dma((4,)),
            dma((2, 20)),
            dma((2, 20)),
            dma((6,)),
        ],
        compiler_params=pltpu.CompilerParams(
            collective_id=0, has_side_effects=True, vmem_limit_bytes=LIMIT
        ),
    )(
        owner_ids.T,
        row_ids.T,
        neighbour_part,
        neighbour_block,
        w_in,
        out_gain,
        tables[0],
        w_pool,
        w_self,
        w_neigh,
        adjacency,
        cotangent,
    )
    table_grad, node_out = pl.pallas_call(
        last_kernel,
        name="last",
        grid=(4,),
        out_shape=(shape((8192, 128), F32), shape((512, 1024), BF16)),
        in_specs=held * 3
        + [
            pl.BlockSpec((2048, 128), lambda c: (c, 0)),
            pl.BlockSpec((128, 1024), lambda c: (c, 0)),
        ],
        out_specs=(
            pl.BlockSpec((2048, 128), lambda c: (c, 0)),
            pl.BlockSpec((128, 1024), lambda c: (c, 0)),
        ),
        scratch_shapes=[vmem((1024, 256), BF16)],
        compiler_params=pltpu.CompilerParams(vmem_limit_bytes=LIMIT),
    )(hot, low, late, sums, node)
    return (node_out, table_grad[None])


def solution(mesh):
    rows = P(("table", "dom"), None)
    placed = (
        P("table", "dom", None),
        rows,
        rows,
        rows,
        rows,
        P(("table", "dom"), None, None, None),
        P(),
        P(),
        P(),
        P(),
        P(),
        rows,
    )
    return jax.shard_map(
        body,
        mesh=mesh,
        in_specs=placed,
        out_specs=(rows, P("table", "dom", None)),
        check_vma=False,
    )
```
